512 devices in a mesh: seq: 128 (over z, y, core), tp: 4 (over x).
Axes of the slice: x: 4, y: 8, z: 8, core: 2. Of those that a mesh axis runs over, the one named last changes fastest.
Arguments:
- state: bfloat16 [16384, 1024], P('seq', 'tp'), may hold values from -16 to 16
- cotangent: float32 [16384, 1024], P('seq', 'tp'), may hold values from -40 to 40
- norm_gain: float32 [1024], replicated, may hold values from 0.5 to 1.5
- w_query: bfloat16 [1024, 1024], P(None, 'tp'), may hold values from -8 to 8
- w_key: bfloat16 [1024, 1024], P(None, 'tp'), may hold values from -1 to 1
- w_value: bfloat16 [1024, 1024], P(None, 'tp'), may hold values from -0.1875 to 0.1875
- w_out: bfloat16 [1024, 1024], P('tp'), may hold values from -1.5 to 1.5
Outputs:
- adjoint: float32 [16384, 1024], P('seq', 'tp')
- residual: float32 [16384, 1024], P('seq', 'tp')
The draws below stay inside these ranges and needn't reach their ends.
All inputs are finite; a program needn't handle non-finite values.
Results may differ from the reference program's by a relative error of at most 0.025.
The reference program's roundings to bfloat16 on the way (of `normed`, `grad_out` and `grad_score`) count: a program that leaves them out, or rounds other values in their place, can miss the bound.
Values may be sent and summed in bfloat16 or wider, within the bound.
A program may use at most 64 MiB of HBM per device.

```python
import math
import jax
import jax.numpy as jnp
from jax import lax

D = 1024
HEADS = 8
HD = 128
WIN = 1024
SSTEP = 4
TOK_DEV = 128
SEQ = 16384


def key_base(key):
    drawn = jax.random.truncated_normal(jax.random.fold_in(key, 31), -6.0, 6.0, (D, D), jnp.float32)
    return drawn / jnp.sqrt(jnp.float32(D))


def draw_w_key(key, part):
    return jnp.clip(key_base(key), -1.0, 1.0).astype(jnp.bfloat16)


def draw_w_query(key, part):
    drawn = jax.random.truncated_normal(jax.random.fold_in(key, 34), -6.0, 6.0, (D, D), jnp.float32) / jnp.sqrt(jnp.float32(D))
    return jnp.clip(drawn, -8.0, 8.0).astype(jnp.bfloat16)


def draw_state(key, part):
    drawn = jax.random.normal(jax.random.fold_in(key, 41), (SEQ, D), jnp.float32)
    return jnp.clip(drawn, -16.0, 16.0).astype(jnp.bfloat16)


def draw_cotangent(key, part):
    position = jnp.arange(SEQ, dtype=jnp.float32)[:, None] / (SEQ - 1)
    drawn = jax.random.normal(jax.random.fold_in(key, 53), (SEQ, D), jnp.float32) * 3.0 ** position
    return jnp.clip(drawn, -40.0, 40.0)


def shard_levels(stream_key, extent, pieces, least, top_value):
    level = 1.0
    for dim, blocks in pieces:
        draws = jax.random.uniform(jax.random.fold_in(jax.random.fold_in(stream_key, 6), dim), (blocks,), jnp.float32, least / len(pieces), top_value / len(pieces))
        level = level * jnp.repeat(jnp.exp(draws), extent[dim] // blocks).reshape((-1,) + (1,) * (len(extent) - 1 - dim))
    return level


def gaussian(key, dims, spread, reach, shards=(), kind=jnp.bfloat16):
    loudness = shard_levels(key, dims, shards, -0.22, 0.18) if shards else 1.0
    array = jax.random.normal(key, dims, jnp.float32) * spread * loudness
    return jnp.minimum(jnp.maximum(array, -reach), reach).astype(kind)


def setup_inputs(seed: int = 0) -> dict:
    seeds = jax.random.split(jax.random.key(seed), 8)
    return {
        "state": draw_state(jax.random.fold_in(seeds[7], 71), 0),
        "cotangent": draw_cotangent(jax.random.fold_in(seeds[7], 71), 0),
        "norm_gain": jnp.clip(1.0 + 0.1 * jax.random.normal(seeds[2], (D,), jnp.float32), 0.5, 1.5),
        "w_query": draw_w_query(jax.random.fold_in(seeds[7], 71), 0),
        "w_key": draw_w_key(jax.random.fold_in(seeds[7], 71), 0),
        "w_value": gaussian(seeds[5], (D, D), D ** -0.5, 0.1875, ((1, 4),)),
        "w_out": gaussian(seeds[6], (D, D), 16 ** -0.5, 1.5, ((0, 4),)),
    }


EPSILON = 1e-05

def lower_solve(factor, values):
    result = []
    for index_i in range(values.shape[0]):
        running = values[index_i]
        for index_j in range(index_i):
            running = running - factor[index_i, index_j] * result[index_j]
        result.append(running / factor[index_i, index_i])
    return jnp.stack(result)

def upper_solve(factor, values):
    length_n = values.shape[0]
    result = [None] * length_n
    for index_i in range(length_n - 1, -1, -1):
        running = values[index_i]
        for index_j in range(index_i + 1, length_n):
            running = running - factor[index_j, index_i] * result[index_j]
        result[index_i] = running / factor[index_i, index_i]
    return jnp.stack(result)

def combine_coefficients(gram_matrix, right_side):
    factor = jnp.linalg.cholesky(gram_matrix)
    return upper_solve(factor, lower_solve(factor, right_side))

def window_valid(first_row, block_rows):
    query_pos = first_row + jnp.arange(block_rows, dtype=jnp.int32)
    key_pos = first_row - WIN // 2 + jnp.arange(block_rows + WIN, dtype=jnp.int32)
    distance = jnp.abs(key_pos[None, :] - query_pos[:, None])
    return (distance <= WIN // 2) & (key_pos[None, :] >= 0) & (key_pos[None, :] < SEQ)

def window_probs(queries_blk, keys_win, valid):
    scores = jnp.einsum('rhe,khe->hrk', queries_blk.astype(jnp.float32), keys_win.astype(jnp.float32)) * (1.0 / math.sqrt(HD))
    row_peak = lax.optimization_barrier(jnp.max(jnp.where(valid[None], scores, -jnp.inf), axis=2, keepdims=True))
    raw_weights = jnp.where(valid[None], jnp.exp(scores - row_peak), 0.0)
    return raw_weights / lax.optimization_barrier(jnp.sum(raw_weights, axis=2, keepdims=True))

def reference(state, cotangent, norm_gain, w_query, w_key, w_value, w_out):
    half_span = WIN // 2
    block_rows = TOK_DEV
    block_count = SEQ // block_rows
    scale_factor = 1.0 / math.sqrt(HD)
    state_full = state.astype(jnp.float32)
    inverse = lax.rsqrt(lax.optimization_barrier(jnp.mean(state_full * state_full, axis=1, keepdims=True)) + EPSILON)
    normed = (state_full * inverse * norm_gain[None, :]).astype(jnp.bfloat16)
    queries = jnp.dot(normed.astype(jnp.float32), w_query.astype(jnp.float32), preferred_element_type=jnp.float32).astype(jnp.bfloat16).reshape(SEQ, HEADS, HD)
    key_vecs = jnp.dot(normed.astype(jnp.float32), w_key.astype(jnp.float32), preferred_element_type=jnp.float32).astype(jnp.bfloat16).reshape(SEQ, HEADS, HD)
    values = jnp.dot(normed.astype(jnp.float32), w_value.astype(jnp.float32), preferred_element_type=jnp.float32).astype(jnp.bfloat16).reshape(SEQ, HEADS, HD)
    padding = ((half_span, half_span), (0, 0), (0, 0))
    keys_pad = jnp.pad(key_vecs, padding)
    values_pad = jnp.pad(values, padding)
    starts = jnp.arange(block_count, dtype=jnp.int32) * block_rows

    def forward_block(first_row):
        queries_blk = lax.dynamic_slice_in_dim(queries, first_row, block_rows, 0)
        keys_win = lax.dynamic_slice_in_dim(keys_pad, first_row, block_rows + WIN, 0)
        values_win = lax.dynamic_slice_in_dim(values_pad, first_row, block_rows + WIN, 0)
        attn_probs = window_probs(queries_blk, keys_win, window_valid(first_row, block_rows))
        return jnp.einsum('hrk,khe->rhe', attn_probs.astype(jnp.bfloat16).astype(jnp.float32), values_win.astype(jnp.float32))
    attended = lax.map(forward_block, starts).reshape(SEQ, HEADS, HD)

    def cell_vjp(vector):
        grad_out = jnp.dot(vector.astype(jnp.bfloat16).astype(jnp.float32), w_out.T.astype(jnp.float32), preferred_element_type=jnp.float32).astype(jnp.bfloat16).reshape(SEQ, HEADS, HD)
        row_corr = lax.optimization_barrier(jnp.sum(grad_out.astype(jnp.float32) * attended, axis=2))

        def block_step(carry, first_row):
            key_acc, value_acc = carry
            queries_blk = lax.dynamic_slice_in_dim(queries, first_row, block_rows, 0)
            keys_win = lax.dynamic_slice_in_dim(keys_pad, first_row, block_rows + WIN, 0)
            values_win = lax.dynamic_slice_in_dim(values_pad, first_row, block_rows + WIN, 0)
            attn_probs = window_probs(queries_blk, keys_win, window_valid(first_row, block_rows))
            out_blk = lax.dynamic_slice_in_dim(grad_out, first_row, block_rows, 0).astype(jnp.float32)
            corr_blk = lax.dynamic_slice_in_dim(row_corr, first_row, block_rows, 0).T
            grad_prob = jnp.einsum('rhe,khe->hrk', out_blk, values_win.astype(jnp.float32))
            grad_score = (scale_factor * attn_probs * (grad_prob - corr_blk[:, :, None])).astype(jnp.bfloat16).astype(jnp.float32)
            grad_query = jnp.einsum('hrk,khe->rhe', grad_score, keys_win.astype(jnp.float32)).astype(jnp.bfloat16)
            key_part = jnp.einsum('hrk,rhe->khe', grad_score, queries_blk.astype(jnp.float32))
            value_part = jnp.einsum('hrk,rhe->khe', attn_probs.astype(jnp.bfloat16).astype(jnp.float32), out_blk)
            key_acc = lax.dynamic_update_slice_in_dim(key_acc, lax.dynamic_slice_in_dim(key_acc, first_row, block_rows + WIN, 0) + key_part, first_row, 0)
            value_acc = lax.dynamic_update_slice_in_dim(value_acc, lax.dynamic_slice_in_dim(value_acc, first_row, block_rows + WIN, 0) + value_part, first_row, 0)
            return ((key_acc, value_acc), grad_query)
        zeros_pad = jnp.zeros((SEQ + WIN, HEADS, HD), jnp.float32)
        (key_acc, value_acc), grad_query = lax.scan(block_step, (zeros_pad, zeros_pad), starts)
        grad_query = grad_query.reshape(SEQ, D)
        grad_key = key_acc[half_span:half_span + SEQ].astype(jnp.bfloat16).reshape(SEQ, D)
        grad_value = value_acc[half_span:half_span + SEQ].astype(jnp.bfloat16).reshape(SEQ, D)
        summed = jnp.dot(grad_query.astype(jnp.float32), w_query.T.astype(jnp.float32), preferred_element_type=jnp.float32)
        summed = summed + jnp.dot(grad_key.astype(jnp.float32), w_key.T.astype(jnp.float32), preferred_element_type=jnp.float32)
        summed = summed + jnp.dot(grad_value.astype(jnp.float32), w_value.T.astype(jnp.float32), preferred_element_type=jnp.float32)
        return inverse * (norm_gain[None, :] * summed)
    krylov = [cotangent]
    for index_n in range(SSTEP):
        krylov.append(cell_vjp(krylov[-1]))
    differences = [krylov[index_n] - krylov[index_n + 1] for index_n in range(SSTEP)]
    gram_matrix = jnp.stack([jnp.stack([jnp.sum(differences[index_a] * differences[index_b]) for index_b in range(SSTEP)]) for index_a in range(SSTEP)])
    right_side = jnp.stack([jnp.sum(differences[index_a] * cotangent) for index_a in range(SSTEP)])
    coefficients = combine_coefficients(gram_matrix, right_side)
    adjoint = coefficients[0] * krylov[0]
    residual = cotangent - coefficients[0] * differences[0]
    for index_n in range(1, SSTEP):
        adjoint = adjoint + coefficients[index_n] * krylov[index_n]
        residual = residual - coefficients[index_n] * differences[index_n]
    return (adjoint, residual)
```

```python
import functools
import math

import jax
import jax.numpy as jnp
from jax import lax
from jax.experimental import pallas as pl
from jax.experimental.pallas import tpu as pltpu
from jax.sharding import PartitionSpec as P

HD = 128
HALF = 512
SSTEP = 4
EPSILON = 1e-05
TOK = 128
CHIP = 2 * TOK
SPAN = CHIP + 2 * HALF
REACH = HALF // CHIP
CHUNKS = 2 * REACH + 1
MSG = TOK + 16
SCALE = 1.0 / math.sqrt(HD)
LOW = -1e30
MESH = pl.DeviceIdType.MESH
F32 = jnp.float32
BF16 = jnp.bfloat16

NT = (((1,), (1,)), ((), ()))
NN = (((1,), (0,)), ((), ()))


def dot(a, b, dims):
    return lax.dot_general(a, b, dims, preferred_element_type=F32)


def wait_for(ref, sem):
    pltpu.make_async_copy(ref, ref, sem).wait()


def kernel(
    sizes,
    state,
    cot,
    gain,
    w_query,
    w_key,
    w_value,
    w_out,
    adj_out,
    res_out,
    w_in,
    w_o,
    gain_v,
    xs,
    xg,
    qkv,
    win,
    att_head,
    att_own,
    stats,
    probs,
    probs_t,
    probs_tb,
    g_msg,
    g_win,
    g_full,
    g_swap,
    rs_send,
    rs_recv,
    kry,
    dif,
    inv_v,
    tiles,
    tile_recv,
    outs,
    sem_load,
    sem_xs_s,
    sem_xs_r,
    sem_xg_s,
    sem_xg_r,
    sem_q_s,
    sem_q_r,
    sem_a_s,
    sem_a_r,
    sem_st_s,
    sem_st_r,
    sem_g_s,
    sem_g_r,
    sem_sw_s,
    sem_sw_r,
    sem_rs_s,
    sem_rs_r,
    sem_t_s,
    sem_t_r,
    sem_out,
):
    n_seq, n_tp, n_y, n_z = sizes
    n_chip = n_seq // 2
    s = lax.axis_index("seq")
    tp = lax.axis_index("tp")
    chip = lax.div(s, 2)
    core = lax.rem(s, 2)
    y = lax.rem(chip, n_y)
    z = lax.div(chip, n_y)
    other = 1 - core
    cols = xs.shape[2]
    pair = (2 * chip + other, tp)

    def at_tp(offset):
        return lax.rem(tp + offset, n_tp)

    def at_chip(offset):
        return lax.rem(chip + offset + n_chip, n_chip)

    tp_far = sorted(range(1, n_tp), key=lambda o: -min(o, n_tp - o))
    halo = [d for k in range(REACH, 0, -1) for d in (-k, k)]
    stage_a = [
        (2 * chip + lax.rem(core + oc, 2), at_tp(ox))
        for ox in range(n_tp)
        for oc in range(2)
        if (ox, oc) != (0, 0)
    ]
    stage_b = [
        (2 * (z * n_y + lax.rem(y + o, n_y)) + core, tp) for o in range(1, n_y)
    ]
    stage_c = [
        (2 * (lax.rem(z + o, n_z) * n_y + y) + core, tp) for o in range(1, n_z)
    ]

    def send(src, dst, ssem, rsem, device):
        pltpu.make_async_remote_copy(
            src_ref=src,
            dst_ref=dst,
            send_sem=ssem,
            recv_sem=rsem,
            device_id=device,
            device_id_type=MESH,
        ).start()

    loads = [
        (state, xs.at[tp]),
        (cot, kry.at[0]),
        (gain, gain_v),
        (w_query, w_in.at[0]),
        (w_key, w_in.at[1]),
        (w_value, w_in.at[2]),
        (w_out, w_o),
    ]
    loading = [
        pltpu.make_async_copy(src, dst, sem_load.at[k])
        for k, (src, dst) in enumerate(loads)
    ]
    for copy in loading:
        copy.start()

    barrier = pltpu.get_barrier_semaphore()
    greeted = stage_a + stage_b + stage_c
    for d in halo:
        for h in range(2):
            greeted.append((2 * at_chip(d) + h, tp))
    for device in greeted:
        pl.semaphore_signal(barrier, inc=1, device_id=device, device_id_type=MESH)
    pl.semaphore_wait(barrier, len(greeted))

    for o in tp_far:
        send(state, xs.at[tp], sem_xs_s, sem_xs_r, (s, at_tp(o)))

    def send_vector(n):
        for o in tp_far:
            send(
                xg.at[n, tp],
                xg.at[n, tp],
                sem_xg_s.at[n],
                sem_xg_r.at[n],
                (s, at_tp(o)),
            )

    loading[1].wait()
    xg[0, tp] = kry[0].astype(BF16)
    send_vector(0)

    loading[0].wait()
    loading[2].wait()
    wait_for(xs.at[pl.ds(0, n_tp - 1)], sem_xs_r)
    total = jnp.zeros((TOK, 1), F32)
    for r in range(n_tp):
        block = xs[r].astype(F32)
        total = total + jnp.sum(block * block, axis=1, keepdims=True)
    inverse = lax.rsqrt(total * (1.0 / (n_tp * cols)) + EPSILON)
    inv_v[...] = jnp.broadcast_to(inverse, inv_v.shape)
    normed = [
        (xs[r].astype(F32) * inverse * gain_v[:, r * cols : (r + 1) * cols]).astype(BF16)
        for r in range(n_tp)
    ]

    own_rows = pl.ds(pl.multiple_of((2 * REACH + core) * TOK, TOK), TOK)

    def slot_rows(d):
        return pl.ds(pl.multiple_of((2 * (REACH - d) + core) * TOK, TOK), TOK)

    for t in (1, 0, 2):
        loading[3 + t].wait()
        acc = jnp.zeros((TOK, 2 * HD), F32)
        for r in range(n_tp):
            acc = acc + dot(normed[r], w_in[t, r * cols : (r + 1) * cols, :], NN)
        acc = acc.astype(BF16)
        for h in range(2):
            qkv[t, h] = acc[:, h * HD : (h + 1) * HD]
        send(
            qkv.at[t, other],
            win.at[t, slot_rows(0)],
            sem_q_s,
            sem_q_r.at[t, REACH],
            pair,
        )
        if t == 1:
            for d in halo:
                for h in range(2):
                    send(
                        qkv.at[t, h],
                        win.at[t, slot_rows(d)],
                        sem_q_s,
                        sem_q_r.at[t, REACH - d],
                        (2 * at_chip(d) + h, tp),
                    )
        win[t, own_rows, :] = qkv[t, core]
    for t in (2, 0):
        for d in halo:
            for h in range(2):
                send(
                    qkv.at[t, h],
                    win.at[t, slot_rows(d)],
                    sem_q_s,
                    sem_q_r.at[t, REACH - d],
                    (2 * at_chip(d) + h, tp),
                )

    def wait_window(t, k):
        rows = TOK if k == REACH else CHIP
        wait_for(win.at[t, pl.ds(0, rows)], sem_q_r.at[t, k])

    arrival = sorted(range(CHUNKS), key=lambda k: abs(k - REACH))
    own = slice(HALF, HALF + CHIP)

    def valid(k):
        row = lax.broadcasted_iota(jnp.int32, (CHIP, CHIP), 0)
        col = lax.broadcasted_iota(jnp.int32, (CHIP, CHIP), 1) + k * CHIP
        place = chip * CHIP - HALF + col
        away = row + HALF - col
        return (
            (away <= HALF)
            & (away >= -HALF)
            & (place >= 0)
            & (place < n_chip * CHIP)
        )

    def part(k):
        return slice(k * CHIP, (k + 1) * CHIP)

    wait_window(0, REACH)
    queries = win[0, own, :]
    peak = jnp.full((CHIP, 1), LOW, F32)
    for k in arrival:
        wait_window(1, k)
        scores = dot(queries, win[1, part(k), :], NT) * SCALE
        scores = jnp.where(valid(k), scores, LOW)
        probs[:, part(k)] = scores
        peak = jnp.maximum(peak, jnp.max(scores, axis=1, keepdims=True))
    mass = jnp.zeros((CHIP, 1), F32)
    for k in arrival:
        raw = jnp.exp(probs[:, part(k)] - peak)
        probs[:, part(k)] = raw
        mass = mass + jnp.sum(raw, axis=1, keepdims=True)
    share = 1.0 / mass
    both = jnp.concatenate(
        [
            jnp.broadcast_to(peak, (CHIP, HD)).T[0:1],
            jnp.broadcast_to(share, (CHIP, HD)).T[0:1],
            jnp.zeros((6, CHIP), F32),
        ],
        axis=0,
    )
    stats[REACH] = both
    for d in halo:
        send(
            stats.at[REACH],
            stats.at[REACH - d],
            sem_st_s,
            sem_st_r,
            (2 * at_chip(d) + core, tp),
        )
    attended = jnp.zeros((CHIP, HD), F32)
    for k in arrival:
        wait_window(2, k)
        weights = probs[:, part(k)] * share
        probs[:, part(k)] = weights * SCALE
        attended = attended + dot(weights.astype(BF16), win[2, part(k), :], NN)
    att_head[...] = attended
    other_half = pl.ds(pl.multiple_of(other * TOK, TOK), TOK)
    own_half = pl.ds(pl.multiple_of(core * TOK, TOK), TOK)
    send(att_head.at[other_half], att_own.at[core], sem_a_s, sem_a_r, pair)
    att_own[core] = att_head[own_half, :]

    def send_grad_out(n):
        wait_for(xg.at[n, pl.ds(0, n_tp - 1)], sem_xg_r.at[n])
        acc = jnp.zeros((TOK, 2 * HD), F32)
        for r in range(n_tp):
            acc = acc + dot(xg[n, r], w_o[:, r * cols : (r + 1) * cols], NT)
        acc = acc.astype(BF16)
        row = lax.broadcasted_iota(jnp.int32, (16, HD), 0)
        for h in range(2):
            grad = acc[:, h * HD : (h + 1) * HD]
            corr = jnp.sum((grad.astype(F32) * att_own[h]).T, axis=0, keepdims=True)
            high = corr.astype(BF16).astype(F32)
            rest = corr - high
            mid = rest.astype(BF16).astype(F32)
            low = rest - mid
            terms = jnp.where(row == 0, high, jnp.where(row == 1, mid, low))
            g_msg[n, h, 0:TOK, :] = grad
            g_msg[n, h, TOK:MSG, :] = terms.astype(BF16)
        send(
            g_msg.at[n, other],
            g_win.at[n, 2 * REACH + core],
            sem_g_s.at[n],
            sem_g_r.at[n, REACH],
            pair,
        )
        for d in halo:
            for h in range(2):
                send(
                    g_msg.at[n, h],
                    g_win.at[n, 2 * (REACH - d) + core],
                    sem_g_s.at[n],
                    sem_g_r.at[n, REACH - d],
                    (2 * at_chip(d) + h, tp),
                )
        g_win[n, 2 * REACH + core] = g_msg[n, core]

    loading[6].wait()
    wait_for(att_own.at[0], sem_a_r)
    send_grad_out(0)

    keys = win[1, own, :]
    values = win[2, own, :]
    wait_for(stats.at[pl.ds(0, CHUNKS - 1)], sem_st_r)
    for k in arrival:
        wait_window(0, k) if k != REACH else None
        scores = dot(keys, win[0, part(k), :], NT) * SCALE
        pair_stats = stats[k]
        scores = jnp.where(valid(k), scores - pair_stats[0:1], LOW)
        weights = jnp.exp(scores) * pair_stats[1:2]
        probs_t[:, part(k)] = weights * SCALE
        probs_tb[:, part(k)] = weights.astype(BF16)

    gain_own = gain_v[:, pl.ds(pl.multiple_of(tp * cols, cols), cols)]

    def product(n, carry):
        def window_grad(k):
            return jnp.concatenate(
                [g_win[n, 2 * k, 0:TOK, :], g_win[n, 2 * k + 1, 0:TOK, :]], axis=0
            )

        def window_corr(k):
            halves = []
            for half in range(2):
                terms = g_win[n, 2 * k + half, TOK:MSG, :].astype(F32)
                halves.append(terms[0:1] + (terms[1:2] + terms[2:3]))
            return jnp.concatenate(halves, axis=1)

        wait_for(g_win.at[n, 0], sem_g_r.at[n, REACH])
        grad = window_grad(REACH)
        corr = jnp.sum(grad.astype(F32) * att_head[...], axis=1, keepdims=True)
        grad_q = jnp.zeros((CHIP, HD), F32)
        for k in range(CHUNKS):
            grad_p = dot(grad, win[2, part(k), :], NT)
            score = (probs[:, part(k)] * (grad_p - corr)).astype(BF16)
            grad_q = grad_q + dot(score, win[1, part(k), :], NN)
        grad_k = jnp.zeros((CHIP, HD), F32)
        grad_v = jnp.zeros((CHIP, HD), F32)
        for k in arrival:
            if k != REACH:
                wait_for(g_win.at[n, pl.ds(0, 2)], sem_g_r.at[n, k])
            grad = window_grad(k)
            grad_p = dot(win[2, own, :], grad, NT)
            score = (probs_t[:, part(k)] * (grad_p - window_corr(k))).astype(BF16)
            grad_k = grad_k + dot(score, win[0, part(k), :], NN)
            grad_v = grad_v + dot(probs_tb[:, part(k)], grad, NN)
        for t, whole in enumerate((grad_q, grad_k, grad_v)):
            whole = whole.astype(BF16)
            first, second = whole[0:TOK], whole[TOK:CHIP]
            mine = core == 0
            g_full[n, core, t] = jnp.where(mine, first, second)
            g_swap[n, t] = jnp.where(mine, second, first)
        send(g_swap.at[n], g_full.at[n, core], sem_sw_s.at[n], sem_sw_r.at[n], pair)
        wait_for(g_swap.at[n], sem_sw_r.at[n])
        grads = [
            jnp.concatenate([g_full[n, 0, t], g_full[n, 1, t]], axis=1) for t in range(3)
        ]

        def partial_sum(o):
            rows = pl.ds(pl.multiple_of(at_tp(o) * cols, cols), cols)
            acc = jnp.zeros((TOK, cols), F32)
            for t in range(3):
                acc = acc + dot(grads[t], w_in[t, rows, :], NT)
            return acc

        for o in tp_far:
            rs_send[n, o - 1] = partial_sum(o).astype(BF16)
            send(
                rs_send.at[n, o - 1],
                rs_recv.at[n, o - 1],
                sem_rs_s.at[n],
                sem_rs_r.at[n],
                (s, at_tp(o)),
            )
        summed = partial_sum(0)
        wait_for(rs_recv.at[n], sem_rs_r.at[n])
        for o in range(1, n_tp):
            summed = summed + rs_recv[n, o - 1].astype(F32)
        vector = inv_v[:, 0:1] * (gain_own * summed)
        kry[n + 1] = vector
        dif[n] = kry[n] - vector

        @pl.when(n < SSTEP - 1)
        def _():
            xg[n + 1, tp] = vector.astype(BF16)
            send_vector(n + 1)
            send_grad_out(n + 1)

        return carry

    lax.fori_loop(0, SSTEP, product, 0)

    tiles[0] = jnp.zeros(tiles.shape[1:], F32)
    place = 0
    where = {}
    for a in range(SSTEP):
        for b in list(range(a + 1)) + ["right"]:
            factor = kry[0] if b == "right" else dif[b]
            row = jnp.sum(dif[a] * factor, axis=0, keepdims=True)
            folded = row[:, 0:HD]
            for start in range(HD, cols, HD):
                folded = folded + row[:, start : start + HD]
            tiles[0, place : place + 1, :] = folded
            where[a, b] = place
            place += 1
    start = 0
    for stage, devices in enumerate((stage_a, stage_b, stage_c)):
        for k, device in enumerate(devices):
            send(
                tiles.at[stage],
                tile_recv.at[start + k],
                sem_t_s,
                sem_t_r.at[stage],
                device,
            )
        wait_for(tile_recv.at[pl.ds(start, len(devices))], sem_t_r.at[stage])
        whole = tiles[stage]
        for k in range(len(devices)):
            whole = whole + tile_recv[start + k]
        tiles[stage + 1] = whole
        start += len(devices)

    def inner(a, b):
        return jnp.sum(
            whole[where[a, b] : where[a, b] + 1], axis=1, keepdims=True
        )

    factor = {}
    for a in range(SSTEP):
        for b in range(a + 1):
            value = inner(a, b)
            for c in range(b):
                value = value - factor[a, c] * factor[b, c]
            factor[a, b] = jnp.sqrt(value) if a == b else value / factor[b, b]
    half = []
    for a in range(SSTEP):
        value = inner(a, "right")
        for b in range(a):
            value = value - factor[a, b] * half[b]
        half.append(value / factor[a, a])
    coef = [None] * SSTEP
    for a in range(SSTEP - 1, -1, -1):
        value = half[a]
        for b in range(a + 1, SSTEP):
            value = value - factor[b, a] * coef[b]
        coef[a] = value / factor[a, a]
    adjoint = coef[0] * kry[0]
    for n in range(1, SSTEP):
        adjoint = adjoint + coef[n] * kry[n]
    outs[0] = adjoint
    out_a = pltpu.make_async_copy(outs.at[0], adj_out, sem_out.at[0])
    out_a.start()
    residual = kry[0]
    for n in range(SSTEP):
        residual = residual - coef[n] * dif[n]
    outs[1] = residual
    out_b = pltpu.make_async_copy(outs.at[1], res_out, sem_out.at[1])
    out_b.start()

    wait_for(xs.at[pl.ds(0, n_tp - 1)], sem_xs_s)
    wait_for(win.at[:, pl.ds(0, (4 * REACH + 1) * TOK)], sem_q_s)
    wait_for(att_own.at[0], sem_a_s)
    wait_for(stats.at[pl.ds(0, CHUNKS - 1)], sem_st_s)
    for n in range(SSTEP):
        wait_for(xg.at[n, pl.ds(0, n_tp - 1)], sem_xg_s.at[n])
        wait_for(g_win.at[n, pl.ds(0, 4 * REACH + 1)], sem_g_s.at[n])
        wait_for(g_swap.at[n], sem_sw_s.at[n])
        wait_for(rs_send.at[n], sem_rs_s.at[n])
    wait_for(tile_recv.at[pl.ds(0, start)], sem_t_s)
    out_a.wait()
    out_b.wait()


def on_device(sizes, state, cotangent, norm_gain, w_query, w_key, w_value, w_out):
    n_seq, n_tp, n_y, n_z = sizes
    tok, cols = state.shape
    width = n_tp * cols
    tile_count = (2 * n_tp - 1) + (n_y - 1) + (n_z - 1)
    dma = pltpu.SemaphoreType.DMA
    scratch = [
        pltpu.VMEM((3, width, 2 * HD), BF16),
        pltpu.VMEM((2 * HD, width), BF16),
        pltpu.VMEM((1, width), F32),
        pltpu.VMEM((n_tp, tok, cols), BF16),
        pltpu.VMEM((SSTEP, n_tp, tok, cols), BF16),
        pltpu.VMEM((3, 2, tok, HD), BF16),
        pltpu.VMEM((3, SPAN, HD), BF16),
        pltpu.VMEM((CHIP, HD), F32),
        pltpu.VMEM((2, tok, HD), F32),
        pltpu.VMEM((CHUNKS, 8, CHIP), F32),
        pltpu.VMEM((CHIP, SPAN), F32),
        pltpu.VMEM((CHIP, SPAN), F32),
        pltpu.VMEM((CHIP, SPAN), BF16),
        pltpu.VMEM((SSTEP, 2, MSG, HD), BF16),
        pltpu.VMEM((SSTEP, 2 * CHUNKS, MSG, HD), BF16),
        pltpu.VMEM((SSTEP, 2, 3, tok, HD), BF16),
        pltpu.VMEM((SSTEP, 3, tok, HD), BF16),
        pltpu.VMEM((SSTEP, n_tp - 1, tok, cols), BF16),
        pltpu.VMEM((SSTEP, n_tp - 1, tok, cols), BF16),
        pltpu.VMEM((SSTEP + 1, tok, cols), F32),
        pltpu.VMEM((SSTEP, tok, cols), F32),
        pltpu.VMEM((tok, HD), F32),
        pltpu.VMEM((4, 16, HD), F32),
        pltpu.VMEM((tile_count, 16, HD), F32),
        pltpu.VMEM((2, tok, cols), F32),
        dma((7,)),
        dma,
        dma,
        dma((SSTEP,)),
        dma((SSTEP,)),
        dma,
        dma((3, CHUNKS)),
        dma,
        dma,
        dma,
        dma,
        dma((SSTEP,)),
        dma((SSTEP, CHUNKS)),
        dma((SSTEP,)),
        dma((SSTEP,)),
        dma((SSTEP,)),
        dma((SSTEP,)),
        dma,
        dma((3,)),
        dma((2,)),
    ]
    anywhere = pl.BlockSpec(memory_space=pl.ANY)
    shape = jax.ShapeDtypeStruct((tok, cols), F32)
    return pl.pallas_call(
        functools.partial(kernel, sizes),
        out_shape=(shape, shape),
        in_specs=[anywhere] * 7,
        out_specs=(anywhere, anywhere),
        scratch_shapes=scratch,
        compiler_params=pltpu.CompilerParams(
            collective_id=0, has_side_effects=True, vmem_limit_bytes=40 * 2**20
        ),
        name="block",
    )(state, cotangent, norm_gain.reshape(1, width), w_query, w_key, w_value, w_out)


def solution(mesh):
    n_seq, n_tp = mesh.shape["seq"], mesh.shape["tp"]
    n_chip = n_seq // 2
    n_y = 1
    while n_y * n_y < n_chip:
        n_y *= 2
    sizes = (n_seq, n_tp, n_y, n_chip // n_y)
    in_specs = (
        P("seq", "tp"),
        P("seq", "tp"),
        P(),
        P(None, "tp"),
        P(None, "tp"),
        P(None, "tp"),
        P("tp", None),
    )
    return jax.shard_map(
        functools.partial(on_device, sizes),
        mesh=mesh,
        in_specs=in_specs,
        out_specs=(P("seq", "tp"), P("seq", "tp")),
        check_vma=False,
    )
```

```python
import functools
import math

import jax
import jax.numpy as jnp
from jax import lax
from jax.experimental import pallas as pl
from jax.experimental.pallas import tpu as pltpu
from jax.sharding import PartitionSpec as P

HD = 128
HALF = 512
SSTEP = 4
EPSILON = 1e-05
TOK = 128
CHIP = 2 * TOK
SPAN = CHIP + 2 * HALF
REACH = HALF // CHIP
CHUNKS = 2 * REACH + 1
BLOCKS = 4
BT = TOK // BLOCKS
SCALE = 1.0 / math.sqrt(HD)
LOW = -1e30
MESH = pl.DeviceIdType.MESH
F32 = jnp.float32
BF16 = jnp.bfloat16

NT = (((1,), (1,)), ((), ()))
NN = (((1,), (0,)), ((), ()))


def dot(a, b, dims):
    return lax.dot_general(a, b, dims, preferred_element_type=F32)


def wait_for(ref, sem):
    pltpu.make_async_copy(ref, ref, sem).wait()


def kernel(
    sizes,
    state,
    cot,
    gain,
    w_query,
    w_key,
    w_value,
    w_out,
    adj_out,
    res_out,
    w_in,
    w_o,
    gain_v,
    xs,
    xg,
    qkv,
    win,
    att_head,
    att_own,
    stats,
    probs,
    probs_t,
    probs_tb,
    g_msg,
    g_win,
    c_msg,
    c_win,
    g_full,
    g_swap,
    rs_acc,
    rs_send,
    rs_recv,
    kry,
    dif,
    inv_v,
    tile,
    rows_out,
    rows_in,
    outs,
    sem_load,
    sem_xs_s,
    sem_xs_r,
    sem_xg_s,
    sem_xg_r,
    sem_q_s,
    sem_q_r,
    sem_a_s,
    sem_a_r,
    sem_st_s,
    sem_st_r,
    sem_g_s,
    sem_g_r,
    sem_c_s,
    sem_c_r,
    sem_sw_s,
    sem_sw_r,
    sem_rs_s,
    sem_rs_r,
    sem_t_s,
    sem_t_r,
    sem_out,
):
    n_seq, n_tp, n_y, n_z = sizes
    n_chip = n_seq // 2
    s = lax.axis_index("seq")
    tp = lax.axis_index("tp")
    chip = lax.div(s, 2)
    core = lax.rem(s, 2)
    y = lax.rem(chip, n_y)
    z = lax.div(chip, n_y)
    other = 1 - core
    cols = xs.shape[2]
    pair = (2 * chip + other, tp)

    def at_tp(offset):
        return lax.rem(tp + offset, n_tp)

    def at_chip(offset):
        return lax.rem(chip + offset + n_chip, n_chip)

    tp_far = sorted(range(1, n_tp), key=lambda o: -min(o, n_tp - o))
    halo = [d for k in range(REACH, 0, -1) for d in (-k, k)]
    blocks = [slice(b * BT, (b + 1) * BT) for b in range(BLOCKS)]
    stage_a = [
        (2 * (z * n_y + lax.rem(y + oy, n_y)) + lax.rem(core + oc, 2), tp)
        for oy in range(n_y)
        for oc in range(2)
        if (oy, oc) != (0, 0)
    ]
    stage_b = [
        (2 * (lax.rem(z + oz, n_z) * n_y + y) + core, at_tp(ox))
        for oz in range(n_z)
        for ox in range(n_tp)
        if (oz, ox) != (0, 0)
    ]

    def send(src, dst, ssem, rsem, device):
        pltpu.make_async_remote_copy(
            src_ref=src,
            dst_ref=dst,
            send_sem=ssem,
            recv_sem=rsem,
            device_id=device,
            device_id_type=MESH,
        ).start()

    loads = [
        (state, xs.at[tp]),
        (cot, kry.at[0]),
        (gain, gain_v),
        (w_query, w_in.at[0]),
        (w_key, w_in.at[1]),
        (w_value, w_in.at[2]),
        (w_out, w_o),
    ]
    loading = [
        pltpu.make_async_copy(src, dst, sem_load.at[k])
        for k, (src, dst) in enumerate(loads)
    ]
    for copy in loading:
        copy.start()

    barrier = pltpu.get_barrier_semaphore()
    greeted = stage_a + stage_b
    for d in halo:
        for h in range(2):
            greeted.append((2 * at_chip(d) + h, tp))
    for device in greeted:
        pl.semaphore_signal(barrier, inc=1, device_id=device, device_id_type=MESH)
    pl.semaphore_wait(barrier, len(greeted))

    for b in range(BLOCKS):
        for o in tp_far:
            send(
                state.at[pl.ds(b * BT, BT)],
                xs.at[tp, pl.ds(b * BT, BT)],
                sem_xs_s,
                sem_xs_r.at[b],
                (s, at_tp(o)),
            )

    def send_vector(n, b):
        for o in tp_far:
            send(
                xg.at[n, tp, pl.ds(b * BT, BT)],
                xg.at[n, tp, pl.ds(b * BT, BT)],
                sem_xg_s.at[n],
                sem_xg_r.at[n, b],
                (s, at_tp(o)),
            )

    def slot_rows(d, b):
        start = (2 * (REACH - d) + core) * TOK + b * BT
        return pl.ds(pl.multiple_of(start, BT), BT)

    def send_window(t, b):
        rows = pl.ds(b * BT, BT)
        send(
            qkv.at[t, other, rows],
            win.at[t, slot_rows(0, b)],
            sem_q_s,
            sem_q_r.at[t, REACH],
            pair,
        )
        for d in halo:
            for h in range(2):
                send(
                    qkv.at[t, h, rows],
                    win.at[t, slot_rows(d, b)],
                    sem_q_s,
                    sem_q_r.at[t, REACH - d],
                    (2 * at_chip(d) + h, tp),
                )
        win[t, slot_rows(0, b), :] = qkv[t, core, b * BT : (b + 1) * BT, :]

    loading[0].wait()
    loading[2].wait()
    for b, rows in enumerate(blocks):
        wait_for(xs.at[pl.ds(0, n_tp - 1), pl.ds(0, BT)], sem_xs_r.at[b])
        if b == BLOCKS - 1:
            loading[1].wait()
            xg[0, tp] = kry[0].astype(BF16)
            for c in range(BLOCKS):
                send_vector(0, c)
        total = jnp.zeros((BT, 1), F32)
        for r in range(n_tp):
            block = xs[r, rows, :].astype(F32)
            total = total + jnp.sum(block * block, axis=1, keepdims=True)
        inverse = lax.rsqrt(total * (1.0 / (n_tp * cols)) + EPSILON)
        inv_v[rows, :] = jnp.broadcast_to(inverse, (BT, HD))
        normed = jnp.concatenate(
            [
                (
                    xs[r, rows, :].astype(F32)
                    * inverse
                    * gain_v[:, r * cols : (r + 1) * cols]
                ).astype(BF16)
                for r in range(n_tp)
            ],
            axis=1,
        )
        for t in (1, 2, 0):
            if b == 0:
                loading[3 + t].wait()
            acc = dot(normed, w_in[t], NN).astype(BF16)
            for h in range(2):
                qkv[t, h, rows, :] = acc[:, h * HD : (h + 1) * HD]
            if t != 0:
                send_window(t, b)
    for b in range(BLOCKS):
        send_window(0, b)

    def wait_window(t, k):
        rows = TOK if k == REACH else CHIP
        wait_for(win.at[t, pl.ds(0, rows)], sem_q_r.at[t, k])

    def send_grad_out(n, b, rows):
        wait_for(xg.at[n, pl.ds(0, n_tp - 1), pl.ds(0, BT)], sem_xg_r.at[n, b])
        acc = jnp.zeros((BT, 2 * HD), F32)
        for r in range(n_tp):
            acc = acc + dot(xg[n, r, rows, :], w_o[:, r * cols : (r + 1) * cols], NT)
        acc = acc.astype(BF16)
        for h in range(2):
            g_msg[n, h, rows, :] = acc[:, h * HD : (h + 1) * HD]
        taken = pl.ds(b * BT, BT)
        send(
            g_msg.at[n, other, taken],
            g_win.at[n, slot_rows(0, b)],
            sem_g_s.at[n],
            sem_g_r.at[n, REACH],
            pair,
        )
        for d in halo:
            for h in range(2):
                send(
                    g_msg.at[n, h, taken],
                    g_win.at[n, slot_rows(d, b)],
                    sem_g_s.at[n],
                    sem_g_r.at[n, REACH - d],
                    (2 * at_chip(d) + h, tp),
                )
        g_win[n, slot_rows(0, b), :] = g_msg[n, core, rows, :]

    def send_corr(n):
        for h in range(2):
            c_msg[n, h] = jnp.sum(
                (g_msg[n, h].astype(F32) * att_own[h]).T, axis=0, keepdims=True
            )
        send(
            c_msg.at[n, other],
            c_win.at[n, 2 * REACH + core],
            sem_c_s.at[n],
            sem_c_r.at[n, REACH],
            pair,
        )
        for d in halo:
            for h in range(2):
                send(
                    c_msg.at[n, h],
                    c_win.at[n, 2 * (REACH - d) + core],
                    sem_c_s.at[n],
                    sem_c_r.at[n, REACH - d],
                    (2 * at_chip(d) + h, tp),
                )
        c_win[n, 2 * REACH + core] = c_msg[n, core]

    loading[6].wait()
    for b, rows in enumerate(blocks):
        send_grad_out(0, b, rows)

    arrival = sorted(range(CHUNKS), key=lambda k: abs(k - REACH))
    own = slice(HALF, HALF + CHIP)

    def valid(k):
        row = lax.broadcasted_iota(jnp.int32, (CHIP, CHIP), 0)
        col = lax.broadcasted_iota(jnp.int32, (CHIP, CHIP), 1) + k * CHIP
        place = chip * CHIP - HALF + col
        away = row + HALF - col
        return (
            (away <= HALF)
            & (away >= -HALF)
            & (place >= 0)
            & (place < n_chip * CHIP)
        )

    def part(k):
        return slice(k * CHIP, (k + 1) * CHIP)

    wait_window(0, REACH)
    queries = win[0, own, :]
    peak = jnp.full((CHIP, 1), LOW, F32)
    for k in arrival:
        wait_window(1, k)
        scores = dot(queries, win[1, part(k), :], NT) * SCALE
        scores = jnp.where(valid(k), scores, LOW)
        probs[:, part(k)] = scores
        peak = jnp.maximum(peak, jnp.max(scores, axis=1, keepdims=True))
    mass = jnp.zeros((CHIP, 1), F32)
    for k in arrival:
        raw = jnp.exp(probs[:, part(k)] - peak)
        probs[:, part(k)] = raw
        mass = mass + jnp.sum(raw, axis=1, keepdims=True)
    share = 1.0 / mass
    both = jnp.concatenate(
        [
            jnp.broadcast_to(peak, (CHIP, HD)).T[0:1],
            jnp.broadcast_to(share, (CHIP, HD)).T[0:1],
            jnp.zeros((6, CHIP), F32),
        ],
        axis=0,
    )
    stats[REACH] = both
    for d in halo:
        send(
            stats.at[REACH],
            stats.at[REACH - d],
            sem_st_s,
            sem_st_r,
            (2 * at_chip(d) + core, tp),
        )
    attended = jnp.zeros((CHIP, HD), F32)
    for k in arrival:
        wait_window(2, k)
        weights = probs[:, part(k)] * share
        probs[:, part(k)] = weights * SCALE
        attended = attended + dot(weights.astype(BF16), win[2, part(k), :], NN)
    att_head[...] = attended
    other_half = pl.ds(pl.multiple_of(other * TOK, TOK), TOK)
    own_half = pl.ds(pl.multiple_of(core * TOK, TOK), TOK)
    send(att_head.at[other_half], att_own.at[core], sem_a_s, sem_a_r, pair)
    att_own[core] = att_head[own_half, :]
    wait_for(att_own.at[0], sem_a_r)
    send_corr(0)

    keys = win[1, own, :]
    values = win[2, own, :]
    wait_for(stats.at[pl.ds(0, CHUNKS - 1)], sem_st_r)
    for k in arrival:
        if k != REACH:
            wait_window(0, k)
        scores = dot(keys, win[0, part(k), :], NT) * SCALE
        pair_stats = stats[k]
        scores = jnp.where(valid(k), scores - pair_stats[0:1], LOW)
        weights = jnp.exp(scores) * pair_stats[1:2]
        probs_t[:, part(k)] = weights * SCALE
        probs_tb[:, part(k)] = weights.astype(BF16)

    gain_own = gain_v[:, pl.ds(pl.multiple_of(tp * cols, cols), cols)]

    def inner_row(a, b):
        row = jnp.sum(dif[a] * (kry[0] if b is None else dif[b]), axis=0, keepdims=True)
        folded = row[:, 0:HD]
        for start in range(HD, cols, HD):
            folded = folded + row[:, start : start + HD]
        return folded

    pairs = [(a, b) for a in range(SSTEP) for b in list(range(a + 1)) + [None]]

    def inner_rows(a):
        for place, (first, second) in enumerate(pairs):
            if first == a:
                tile[place : place + 1, :] = inner_row(first, second)

    tile[...] = jnp.zeros(tile.shape, F32)

    def product(n, carry):
        def give_back(t, whole):
            whole = whole.astype(BF16)
            first, second = whole[0:TOK], whole[TOK:CHIP]
            mine = core == 0
            g_full[n, core, t] = jnp.where(mine, first, second)
            g_swap[n, t] = jnp.where(mine, second, first)

        def both_heads(t):
            return jnp.concatenate([g_full[n, 0, t], g_full[n, 1, t]], axis=1)

        def tp_rows(o):
            return pl.ds(pl.multiple_of(at_tp(o) * cols, cols), cols)

        wait_for(g_win.at[n, pl.ds(0, TOK)], sem_g_r.at[n, REACH])
        grad = g_win[n, own, :]
        corr = jnp.sum(grad.astype(F32) * att_head[...], axis=1, keepdims=True)
        grad_q = jnp.zeros((CHIP, HD), F32)
        for k in range(CHUNKS):
            grad_p = dot(grad, win[2, part(k), :], NT)
            score = (probs[:, part(k)] * (grad_p - corr)).astype(BF16)
            grad_q = grad_q + dot(score, win[1, part(k), :], NN)
        give_back(0, grad_q)
        send(
            g_swap.at[n, pl.ds(0, 1)],
            g_full.at[n, core, pl.ds(0, 1)],
            sem_sw_s.at[n],
            sem_sw_r.at[n, 0],
            pair,
        )
        grad_k = jnp.zeros((CHIP, HD), F32)
        grad_v = jnp.zeros((CHIP, HD), F32)
        for k in arrival:
            if k != REACH:
                wait_for(g_win.at[n, pl.ds(0, CHIP)], sem_g_r.at[n, k])
            wait_for(c_win.at[n, pl.ds(0, 1 if k == REACH else 2)], sem_c_r.at[n, k])
            grad = g_win[n, part(k), :]
            corr = jnp.concatenate([c_win[n, 2 * k], c_win[n, 2 * k + 1]], axis=1)
            grad_p = dot(values, grad, NT)
            score = (probs_t[:, part(k)] * (grad_p - corr)).astype(BF16)
            grad_k = grad_k + dot(score, win[0, part(k), :], NN)
            grad_v = grad_v + dot(probs_tb[:, part(k)], grad, NN)
            if k == REACH:
                wait_for(g_swap.at[n, pl.ds(0, 1)], sem_sw_r.at[n, 0])
                for o in range(n_tp):
                    rs_acc[o] = dot(both_heads(0), w_in[0, tp_rows(o), :], NT)
        give_back(1, grad_k)
        give_back(2, grad_v)
        send(
            g_swap.at[n, pl.ds(1, 2)],
            g_full.at[n, core, pl.ds(1, 2)],
            sem_sw_s.at[n],
            sem_sw_r.at[n, 1],
            pair,
        )
        wait_for(g_swap.at[n, pl.ds(1, 2)], sem_sw_r.at[n, 1])
        late = [both_heads(1), both_heads(2)]

        def partial_sum(o):
            acc = rs_acc[o]
            for t in range(2):
                acc = acc + dot(late[t], w_in[1 + t, tp_rows(o), :], NT)
            return acc

        def send_sum(o, b):
            send(
                rs_send.at[n, o - 1, pl.ds(b * BT, BT)],
                rs_recv.at[n, o - 1, pl.ds(b * BT, BT)],
                sem_rs_s.at[n],
                sem_rs_r.at[n, b],
                (s, at_tp(o)),
            )

        for o in tp_far:
            rs_send[n, o - 1] = partial_sum(o).astype(BF16)
            send_sum(o, 0)
        for b in range(1, BLOCKS):
            for o in tp_far:
                send_sum(o, b)
        rs_acc[0] = partial_sum(0)
        for b, rows in enumerate(blocks):
            wait_for(
                rs_recv.at[n, pl.ds(0, n_tp - 1), pl.ds(0, BT)], sem_rs_r.at[n, b]
            )
            summed = rs_acc[0, rows, :]
            for o in range(1, n_tp):
                summed = summed + rs_recv[n, o - 1, rows, :].astype(F32)
            inverse = jnp.concatenate([inv_v[rows, :]] * (cols // HD), axis=1)
            vector = inverse * (gain_own * summed)

            @pl.when(n < SSTEP - 1)
            def _():
                xg[n + 1, tp, rows, :] = vector.astype(BF16)
                send_vector(n + 1, b)

            kry[n + 1, rows, :] = vector
            dif[n, rows, :] = kry[n, rows, :] - vector

        @pl.when(n < SSTEP - 1)
        def _():
            for b, rows in enumerate(blocks):
                send_grad_out(n + 1, b, rows)
            send_corr(n + 1)

        for a in range(SSTEP):

            @pl.when(n == a)
            def _():
                inner_rows(a)

        return carry

    lax.fori_loop(0, SSTEP, product, 0)

    square = jnp.concatenate(
        [tile[...], jnp.zeros((HD - tile.shape[0], HD), F32)], axis=0
    )
    whole = jnp.sum(square.T, axis=0, keepdims=True)
    start = 0
    for stage, devices in enumerate((stage_a, stage_b)):
        rows_out[stage] = whole
        for k, device in enumerate(devices):
            send(
                rows_out.at[stage],
                rows_in.at[start + k],
                sem_t_s,
                sem_t_r.at[stage],
                device,
            )
        wait_for(rows_in.at[pl.ds(start, len(devices))], sem_t_r.at[stage])
        whole = whole + jnp.sum(rows_in[start : start + len(devices)], axis=0)
        start += len(devices)
    spread = jnp.broadcast_to(whole, (HD, HD)).T

    def inner(a, b):
        place = pairs.index((a, b))
        return spread[place : place + 1]

    factor = {}
    for a in range(SSTEP):
        for b in range(a + 1):
            value = inner(a, b)
            for c in range(b):
                value = value - factor[a, c] * factor[b, c]
            factor[a, b] = jnp.sqrt(value) if a == b else value / factor[b, b]
    half = []
    for a in range(SSTEP):
        value = inner(a, None)
        for b in range(a):
            value = value - factor[a, b] * half[b]
        half.append(value / factor[a, a])
    coef = [None] * SSTEP
    for a in range(SSTEP - 1, -1, -1):
        value = half[a]
        for b in range(a + 1, SSTEP):
            value = value - factor[b, a] * coef[b]
        coef[a] = value / factor[a, a]
    coef = [jnp.concatenate([c] * (cols // HD), axis=1) for c in coef]
    adjoint = coef[0] * kry[0]
    for n in range(1, SSTEP):
        adjoint = adjoint + coef[n] * kry[n]
    outs[0] = adjoint
    out_a = pltpu.make_async_copy(outs.at[0], adj_out, sem_out.at[0])
    out_a.start()
    residual = kry[0]
    for n in range(SSTEP):
        residual = residual - coef[n] * dif[n]
    outs[1] = residual
    out_b = pltpu.make_async_copy(outs.at[1], res_out, sem_out.at[1])
    out_b.start()

    sent = 4 * REACH + 1
    wait_for(xs.at[pl.ds(0, n_tp - 1)], sem_xs_s)
    wait_for(win.at[:, pl.ds(0, sent * TOK)], sem_q_s)
    wait_for(att_own.at[0], sem_a_s)
    wait_for(stats.at[pl.ds(0, CHUNKS - 1)], sem_st_s)
    for n in range(SSTEP):
        wait_for(xg.at[n, pl.ds(0, n_tp - 1)], sem_xg_s.at[n])
        wait_for(g_win.at[n, pl.ds(0, sent * TOK)], sem_g_s.at[n])
        wait_for(c_win.at[n, pl.ds(0, sent)], sem_c_s.at[n])
        wait_for(g_swap.at[n], sem_sw_s.at[n])
        wait_for(rs_send.at[n], sem_rs_s.at[n])
    wait_for(rows_in, sem_t_s)
    out_a.wait()
    out_b.wait()


def on_device(sizes, state, cotangent, norm_gain, w_query, w_key, w_value, w_out):
    n_seq, n_tp, n_y, n_z = sizes
    tok, cols = state.shape
    width = n_tp * cols
    row_count = (2 * n_y - 1) + (n_z * n_tp - 1)
    dma = pltpu.SemaphoreType.DMA
    scratch = [
        pltpu.VMEM((3, width, 2 * HD), BF16),
        pltpu.VMEM((2 * HD, width), BF16),
        pltpu.VMEM((1, width), F32),
        pltpu.VMEM((n_tp, tok, cols), BF16),
        pltpu.VMEM((SSTEP, n_tp, tok, cols), BF16),
        pltpu.VMEM((3, 2, tok, HD), BF16),
        pltpu.VMEM((3, SPAN, HD), BF16),
        pltpu.VMEM((CHIP, HD), F32),
        pltpu.VMEM((2, tok, HD), F32),
        pltpu.VMEM((CHUNKS, 8, CHIP), F32),
        pltpu.VMEM((CHIP, SPAN), F32),
        pltpu.VMEM((CHIP, SPAN), F32),
        pltpu.VMEM((CHIP, SPAN), BF16),
        pltpu.VMEM((SSTEP, 2, tok, HD), BF16),
        pltpu.VMEM((SSTEP, SPAN, HD), BF16),
        pltpu.VMEM((SSTEP, 2, 1, HD), F32),
        pltpu.VMEM((SSTEP, 2 * CHUNKS, 1, HD), F32),
        pltpu.VMEM((SSTEP, 2, 3, tok, HD), BF16),
        pltpu.VMEM((SSTEP, 3, tok, HD), BF16),
        pltpu.VMEM((n_tp, tok, cols), F32),
        pltpu.VMEM((SSTEP, n_tp - 1, tok, cols), BF16),
        pltpu.VMEM((SSTEP, n_tp - 1, tok, cols), BF16),
        pltpu.VMEM((SSTEP + 1, tok, cols), F32),
        pltpu.VMEM((SSTEP, tok, cols), F32),
        pltpu.VMEM((tok, HD), F32),
        pltpu.VMEM((16, HD), F32),
        pltpu.VMEM((2, 1, HD), F32),
        pltpu.VMEM((row_count, 1, HD), F32),
        pltpu.VMEM((2, tok, cols), F32),
        dma((7,)),
        dma,
        dma((BLOCKS,)),
        dma((SSTEP,)),
        dma((SSTEP, BLOCKS)),
        dma,
        dma((3, CHUNKS)),
        dma,
        dma,
        dma,
        dma,
        dma((SSTEP,)),
        dma((SSTEP, CHUNKS)),
        dma((SSTEP,)),
        dma((SSTEP, CHUNKS)),
        dma((SSTEP,)),
        dma((SSTEP, 2)),
        dma((SSTEP,)),
        dma((SSTEP, BLOCKS)),
        dma,
        dma((2,)),
        dma((2,)),
    ]
    anywhere = pl.BlockSpec(memory_space=pl.ANY)
    shape = jax.ShapeDtypeStruct((tok, cols), F32)
    return pl.pallas_call(
        functools.partial(kernel, sizes),
        out_shape=(shape, shape),
        in_specs=[anywhere] * 7,
        out_specs=(anywhere, anywhere),
        scratch_shapes=scratch,
        compiler_params=pltpu.CompilerParams(
            collective_id=0, has_side_effects=True, vmem_limit_bytes=63 * 2**20
        ),
        name="block",
    )(state, cotangent, norm_gain.reshape(1, width), w_query, w_key, w_value, w_out)


def solution(mesh):
    n_seq, n_tp = mesh.shape["seq"], mesh.shape["tp"]
    n_chip = n_seq // 2
    n_y = 1
    while n_y * n_y < n_chip:
        n_y *= 2
    sizes = (n_seq, n_tp, n_y, n_chip // n_y)
    in_specs = (
        P("seq", "tp"),
        P("seq", "tp"),
        P(),
        P(None, "tp"),
        P(None, "tp"),
        P(None, "tp"),
        P("tp", None),
    )
    return jax.shard_map(
        functools.partial(on_device, sizes),
        mesh=mesh,
        in_specs=in_specs,
        out_specs=(P("seq", "tp"), P("seq", "tp")),
        check_vma=False,
    )
```

```python
import functools
import math

import jax
import jax.numpy as jnp
from jax import lax
from jax.experimental import pallas as pl
from jax.experimental.pallas import tpu as pltpu
from jax.sharding import PartitionSpec as P

HD = 128
HALF = 512
SSTEP = 4
EPSILON = 1e-05
TOK = 128
CHIP = 2 * TOK
SPAN = CHIP + 2 * HALF
REACH = HALF // CHIP
CHUNKS = 2 * REACH + 1
BLOCKS = 4
BT = TOK // BLOCKS
SCALE = 1.0 / math.sqrt(HD)
LOW = -1e30
MESH = pl.DeviceIdType.MESH
F32 = jnp.float32
BF16 = jnp.bfloat16

NT = (((1,), (1,)), ((), ()))
NN = (((1,), (0,)), ((), ()))


def dot(a, b, dims):
    return lax.dot_general(a, b, dims, preferred_element_type=F32)


def wait_for(ref, sem):
    pltpu.make_async_copy(ref, ref, sem).wait()


def kernel(
    sizes,
    state,
    cot,
    gain,
    w_query,
    w_key,
    w_value,
    w_out,
    adj_out,
    res_out,
    w_q,
    w_kv,
    w_o,
    gain_v,
    xs,
    normed_v,
    xg,
    qkv,
    win,
    att_head,
    att_own,
    stats,
    probs,
    probs_t,
    probs_tb,
    g_msg,
    g_win,
    c_msg,
    c_win,
    g_full,
    g_swap,
    kv_acc,
    rs_acc,
    rs_send,
    rs_recv,
    kry,
    dif,
    inv_v,
    tile,
    rows_out,
    rows_in,
    sem_load,
    sem_xs_s,
    sem_xs_r,
    sem_xg_s,
    sem_xg_r,
    sem_q_s,
    sem_kv_r,
    sem_q_r,
    sem_a_s,
    sem_a_r,
    sem_st_s,
    sem_st_r,
    sem_g_s,
    sem_g_r,
    sem_c_s,
    sem_c_r,
    sem_sw_s,
    sem_sw_r,
    sem_rs_s,
    sem_rs_r,
    sem_t_s,
    sem_t_r,
):
    n_seq, n_tp, n_y, n_z = sizes
    n_chip = n_seq // 2
    s = lax.axis_index("seq")
    tp = lax.axis_index("tp")
    chip = lax.div(s, 2)
    core = lax.rem(s, 2)
    y = lax.rem(chip, n_y)
    z = lax.div(chip, n_y)
    other = 1 - core
    cols = xs.shape[2]
    pair = (2 * chip + other, tp)

    def at_tp(offset):
        return lax.rem(tp + offset, n_tp)

    def at_chip(offset):
        return lax.rem(chip + offset + n_chip, n_chip)

    tp_far = sorted(range(1, n_tp), key=lambda o: -min(o, n_tp - o))
    near = (-1, 1)
    halo = [d for k in range(REACH, 0, -1) for d in (-k, k)]
    blocks = [slice(b * BT, (b + 1) * BT) for b in range(BLOCKS)]
    stage_a = [
        (2 * (z * n_y + lax.rem(y + oy, n_y)) + lax.rem(core + oc, 2), tp)
        for oy in range(n_y)
        for oc in range(2)
        if (oy, oc) != (0, 0)
    ]
    stage_b = [
        (2 * (lax.rem(z + oz, n_z) * n_y + y) + core, at_tp(ox))
        for oz in range(n_z)
        for ox in range(n_tp)
        if (oz, ox) != (0, 0)
    ]

    def send(src, dst, ssem, rsem, device):
        pltpu.make_async_remote_copy(
            src_ref=src,
            dst_ref=dst,
            send_sem=ssem,
            recv_sem=rsem,
            device_id=device,
            device_id_type=MESH,
        ).start()

    barrier = pltpu.get_barrier_semaphore()
    greeted = stage_a + stage_b
    for d in halo:
        for h in range(2):
            greeted.append((2 * at_chip(d) + h, tp))
    for device in greeted:
        pl.semaphore_signal(barrier, inc=1, device_id=device, device_id_type=MESH)

    loads = [
        (cot, kry.at[0]),
        (state, xs.at[tp]),
        (gain, gain_v),
    ]
    for h in range(2):
        for t, source in enumerate((w_key, w_value)):
            loads.append(
                (
                    source.at[:, pl.ds(h * HD, HD)],
                    w_kv.at[h, :, pl.ds(t * HD, HD)],
                )
            )
    loads += [(w_query, w_q), (w_out, w_o)]
    loading = [
        pltpu.make_async_copy(src, dst, sem_load.at[k])
        for k, (src, dst) in enumerate(loads)
    ]
    for copy in loading:
        copy.start()
    pl.semaphore_wait(barrier, len(greeted))

    for b in range(BLOCKS):
        for o in tp_far:
            send(
                state.at[pl.ds(b * BT, BT)],
                xs.at[tp, pl.ds(b * BT, BT)],
                sem_xs_s,
                sem_xs_r.at[b],
                (s, at_tp(o)),
            )

    def send_vector(n, b):
        for o in tp_far:
            send(
                xg.at[n, tp, pl.ds(b * BT, BT)],
                xg.at[n, tp, pl.ds(b * BT, BT)],
                sem_xg_s.at[n],
                sem_xg_r.at[n, b],
                (s, at_tp(o)),
            )

    def slot_rows(d, b):
        start = (2 * (REACH - d) + core) * TOK + b * BT
        return pl.ds(pl.multiple_of(start, BT), BT)

    def send_window(t, count, start, size, rsem):
        rows = pl.ds(start, size)
        place = pl.ds(t, count)

        def target(d):
            first = (2 * (REACH - d) + core) * TOK + start
            return win.at[place, pl.ds(pl.multiple_of(first, BT), size)]

        send(qkv.at[other, place, rows], target(0), sem_q_s, rsem(REACH), pair)
        for d in near:
            for h in range(2):
                send(
                    qkv.at[h, place, rows],
                    target(d),
                    sem_q_s,
                    rsem(REACH - d),
                    (2 * at_chip(d) + h, tp),
                )
        own_rows = pl.ds(
            pl.multiple_of((2 * REACH + core) * TOK + start, BT), size
        )
        for k in range(t, t + count):
            win[k, own_rows, :] = qkv[core, k, start : start + size, :]

    def wait_kv(k, b):
        rows = BT if k == REACH else 2 * BT
        wait_for(win.at[pl.ds(1, 2), pl.ds(0, rows)], sem_kv_r.at[k, b])

    def wait_q(k):
        wait_for(win.at[0, pl.ds(0, TOK if k == REACH else CHIP)], sem_q_r.at[k])

    def pass_on(t, count, starts, size, rsem):
        for d in near:
            k = REACH - d
            for start in starts:
                first = k * CHIP + start
                send(
                    win.at[pl.ds(t, count), pl.ds(first, size)],
                    win.at[pl.ds(t, count), pl.ds(first - d * CHIP, size)],
                    sem_q_s,
                    rsem(k - d),
                    (2 * at_chip(d) + core, tp),
                )

    loading[2].wait()
    for b, rows in enumerate(blocks):
        wait_for(xs.at[pl.ds(0, n_tp - 1), pl.ds(0, BT)], sem_xs_r.at[b])
        if b == 0:
            loading[0].wait()
            loading[1].wait()
        if b == BLOCKS - 1:
            xg[0, tp] = kry[0].astype(BF16)
            for c in range(BLOCKS):
                send_vector(0, c)
        total = jnp.zeros((BT, 1), F32)
        for r in range(n_tp):
            block = xs[r, rows, :].astype(F32)
            total = total + jnp.sum(block * block, axis=1, keepdims=True)
        inverse = lax.rsqrt(total * (1.0 / (n_tp * cols)) + EPSILON)
        inv_v[rows, :] = jnp.broadcast_to(inverse, (BT, HD))
        normed = jnp.concatenate(
            [
                (
                    xs[r, rows, :].astype(F32)
                    * inverse
                    * gain_v[:, r * cols : (r + 1) * cols]
                ).astype(BF16)
                for r in range(n_tp)
            ],
            axis=1,
        )
        normed_v[rows, :] = normed
        for h in range(2):
            if b == 0:
                loading[3 + 2 * h].wait()
                loading[4 + 2 * h].wait()
            acc = dot(normed, w_kv[h], NN).astype(BF16)
            for t in range(2):
                qkv[h, 1 + t, rows, :] = acc[:, t * HD : (t + 1) * HD]
        send_window(1, 2, b * BT, BT, lambda k, b=b: sem_kv_r.at[k, b])
    loading[7].wait()
    acc = dot(normed_v[...], w_q[...], NN).astype(BF16)
    for h in range(2):
        qkv[h, 0] = acc[:, h * HD : (h + 1) * HD]
    send_window(0, 1, 0, TOK, lambda k: sem_q_r.at[k])
    for b in range(BLOCKS):
        for d in near:
            wait_kv(REACH - d, b)
        pass_on(1, 2, [b * BT, TOK + b * BT], BT, lambda k, b=b: sem_kv_r.at[k, b])

    def send_grad_out(n, b, rows):
        wait_for(xg.at[n, pl.ds(0, n_tp - 1), pl.ds(0, BT)], sem_xg_r.at[n, b])
        acc = jnp.zeros((BT, 2 * HD), F32)
        for r in range(n_tp):
            acc = acc + dot(xg[n, r, rows, :], w_o[:, r * cols : (r + 1) * cols], NT)
        acc = acc.astype(BF16)
        for h in range(2):
            g_msg[n, h, rows, :] = acc[:, h * HD : (h + 1) * HD]
        taken = pl.ds(b * BT, BT)
        send(
            g_msg.at[n, other, taken],
            g_win.at[n, slot_rows(0, b)],
            sem_g_s.at[n],
            sem_g_r.at[n, REACH],
            pair,
        )
        for d in halo:
            for h in range(2):
                send(
                    g_msg.at[n, h, taken],
                    g_win.at[n, slot_rows(d, b)],
                    sem_g_s.at[n],
                    sem_g_r.at[n, REACH - d],
                    (2 * at_chip(d) + h, tp),
                )
        g_win[n, slot_rows(0, b), :] = g_msg[n, core, rows, :]

    def send_corr(n):
        for h in range(2):
            c_msg[n, h] = jnp.sum(
                (g_msg[n, h].astype(F32) * att_own[h]).T, axis=0, keepdims=True
            )
        send(
            c_msg.at[n, other],
            c_win.at[n, 2 * REACH + core],
            sem_c_s.at[n],
            sem_c_r.at[n, REACH],
            pair,
        )
        for d in halo:
            for h in range(2):
                send(
                    c_msg.at[n, h],
                    c_win.at[n, 2 * (REACH - d) + core],
                    sem_c_s.at[n],
                    sem_c_r.at[n, REACH - d],
                    (2 * at_chip(d) + h, tp),
                )
        c_win[n, 2 * REACH + core] = c_msg[n, core]

    arrival = sorted(range(CHUNKS), key=lambda k: abs(k - REACH))
    own = slice(HALF, HALF + CHIP)

    def valid(k):
        row = lax.broadcasted_iota(jnp.int32, (CHIP, CHIP), 0)
        col = lax.broadcasted_iota(jnp.int32, (CHIP, CHIP), 1) + k * CHIP
        place = chip * CHIP - HALF + col
        away = row + HALF - col
        return (
            (away <= HALF)
            & (away >= -HALF)
            & (place >= 0)
            & (place < n_chip * CHIP)
        )

    def part(k):
        return slice(k * CHIP, (k + 1) * CHIP)

    def scores_of(k, peak):
        scores = dot(win[0, own, :], win[1, part(k), :], NT) * SCALE
        scores = jnp.where(valid(k), scores, LOW)
        probs[:, part(k)] = scores
        return jnp.maximum(peak, jnp.max(scores, axis=1, keepdims=True))

    wait_q(REACH)
    for b in range(BLOCKS):
        wait_kv(REACH, b)
    peak = jnp.full((CHIP, 1), LOW, F32)
    for k in arrival[:3]:
        peak = scores_of(k, peak)
    for d in near:
        wait_q(REACH - d)
    pass_on(0, 1, [0], CHIP, lambda k: sem_q_r.at[k])
    loading[8].wait()
    for b, rows in enumerate(blocks):
        send_grad_out(0, b, rows)
    for k in arrival[3:]:
        for b in range(BLOCKS):
            wait_kv(k, b)
        peak = scores_of(k, peak)
    mass = jnp.zeros((CHIP, 1), F32)
    for k in arrival:
        raw = jnp.exp(probs[:, part(k)] - peak)
        probs[:, part(k)] = raw
        mass = mass + jnp.sum(raw, axis=1, keepdims=True)
    share = 1.0 / mass
    both = jnp.concatenate(
        [
            jnp.broadcast_to(peak, (CHIP, HD)).T[0:1],
            jnp.broadcast_to(share, (CHIP, HD)).T[0:1],
            jnp.zeros((6, CHIP), F32),
        ],
        axis=0,
    )
    stats[REACH] = both
    for d in halo:
        send(
            stats.at[REACH],
            stats.at[REACH - d],
            sem_st_s,
            sem_st_r,
            (2 * at_chip(d) + core, tp),
        )
    attended = jnp.zeros((CHIP, HD), F32)
    for k in arrival:
        weights = probs[:, part(k)] * share
        probs[:, part(k)] = weights * SCALE
        attended = attended + dot(weights.astype(BF16), win[2, part(k), :], NN)
    att_head[...] = attended
    other_half = pl.ds(pl.multiple_of(other * TOK, TOK), TOK)
    own_half = pl.ds(pl.multiple_of(core * TOK, TOK), TOK)
    send(att_head.at[other_half], att_own.at[core], sem_a_s, sem_a_r, pair)
    att_own[core] = att_head[own_half, :]
    wait_for(att_own.at[0], sem_a_r)
    send_corr(0)

    keys = win[1, own, :]
    wait_for(stats.at[pl.ds(0, CHUNKS - 1)], sem_st_r)
    for k in arrival:
        if abs(k - REACH) == 2:
            wait_q(k)
        scores = dot(keys, win[0, part(k), :], NT) * SCALE
        pair_stats = stats[k]
        scores = jnp.where(valid(k), scores - pair_stats[0:1], LOW)
        weights = jnp.exp(scores) * pair_stats[1:2]
        probs_t[:, part(k)] = weights * SCALE
        probs_tb[:, part(k)] = weights.astype(BF16)

    gain_own = gain_v[:, pl.ds(pl.multiple_of(tp * cols, cols), cols)]

    def inner_row(a, b):
        row = jnp.sum(dif[a] * (kry[0] if b is None else dif[b]), axis=0, keepdims=True)
        folded = row[:, 0:HD]
        for start in range(HD, cols, HD):
            folded = folded + row[:, start : start + HD]
        return folded

    pairs = [(a, b) for a in range(SSTEP) for b in list(range(a + 1)) + [None]]

    def inner_rows(a):
        for place, (first, second) in enumerate(pairs):
            if first == a:
                tile[place : place + 1, :] = inner_row(first, second)

    tile[...] = jnp.zeros(tile.shape, F32)

    def product(n, carry):
        def give_back(t, whole):
            whole = whole.astype(BF16)
            first, second = whole[0:TOK], whole[TOK:CHIP]
            mine = core == 0
            g_full[n, core, t] = jnp.where(mine, first, second)
            g_swap[n, t] = jnp.where(mine, second, first)

        def both_heads(t):
            return jnp.concatenate([g_full[n, 0, t], g_full[n, 1, t]], axis=1)

        def tp_rows(o):
            return pl.ds(pl.multiple_of(at_tp(o) * cols, cols), cols)

        wait_for(g_win.at[n, pl.ds(0, TOK)], sem_g_r.at[n, REACH])
        grad = g_win[n, own, :]
        corr = jnp.sum(grad.astype(F32) * att_head[...], axis=1, keepdims=True)
        grad_q = jnp.zeros((CHIP, HD), F32)
        for k in range(CHUNKS):
            grad_p = dot(grad, win[2, part(k), :], NT)
            score = (probs[:, part(k)] * (grad_p - corr)).astype(BF16)
            grad_q = grad_q + dot(score, win[1, part(k), :], NN)
        give_back(0, grad_q)
        send(
            g_swap.at[n, pl.ds(0, 1)],
            g_full.at[n, core, pl.ds(0, 1)],
            sem_sw_s.at[n],
            sem_sw_r.at[n, 0],
            pair,
        )
        def key_side(k, values, wide, low):
            grad = g_win[n, part(k), :]
            corr = jnp.concatenate([c_win[n, 2 * k], c_win[n, 2 * k + 1]], axis=1)
            score = (wide * (dot(values, grad, NT) - corr)).astype(BF16)
            return dot(score, win[0, part(k), :], NN), dot(low, grad, NN)

        def wait_grad(k):
            if k != REACH:
                wait_for(g_win.at[n, pl.ds(0, CHIP)], sem_g_r.at[n, k])
            wait_for(c_win.at[n, pl.ds(0, 1 if k == REACH else 2)], sem_c_r.at[n, k])

        for place, k in enumerate(arrival[:3]):
            wait_grad(k)
            grad_k, grad_v = key_side(
                k, win[2, own, :], probs_t[:, part(k)], probs_tb[:, part(k)]
            )
            if place == 0:
                kv_acc[0] = grad_k
                kv_acc[1] = grad_v
                wait_for(g_swap.at[n, pl.ds(0, 1)], sem_sw_r.at[n, 0])
                for o in range(n_tp):
                    rs_acc[o] = dot(both_heads(0), w_q[tp_rows(o), :], NT)
            else:
                kv_acc[0] += grad_k
                kv_acc[1] += grad_v
        for k in arrival[3:]:
            wait_grad(k)
        for token_core in (other, core):
            taken = pl.ds(pl.multiple_of(token_core * TOK, TOK), TOK)
            window = pl.ds(pl.multiple_of(HALF + token_core * TOK, TOK), TOK)
            sums = [kv_acc[0, taken, :], kv_acc[1, taken, :]]
            for k in arrival[3:]:
                grad_k, grad_v = key_side(
                    k,
                    win[2, window, :],
                    probs_t[taken, part(k)],
                    probs_tb[taken, part(k)],
                )
                sums = [sums[0] + grad_k, sums[1] + grad_v]
            for t in range(2):
                if token_core is other:
                    g_swap[n, 1 + t] = sums[t].astype(BF16)
                else:
                    g_full[n, core, 1 + t] = sums[t].astype(BF16)
            if token_core is other:
                send(
                    g_swap.at[n, pl.ds(1, 2)],
                    g_full.at[n, core, pl.ds(1, 2)],
                    sem_sw_s.at[n],
                    sem_sw_r.at[n, 1],
                    pair,
                )

        def partial_sum(o, head):
            late = jnp.concatenate([g_full[n, head, 1], g_full[n, head, 2]], axis=1)
            return rs_acc[o] + dot(late, w_kv[head, tp_rows(o), :], NT)

        for o in range(n_tp):
            rs_acc[o] = partial_sum(o, core)
        wait_for(g_swap.at[n, pl.ds(1, 2)], sem_sw_r.at[n, 1])

        def send_sum(o, b):
            send(
                rs_send.at[n, o - 1, pl.ds(b * BT, BT)],
                rs_recv.at[n, o - 1, pl.ds(b * BT, BT)],
                sem_rs_s.at[n],
                sem_rs_r.at[n, b],
                (s, at_tp(o)),
            )

        for o in tp_far:
            rs_send[n, o - 1] = partial_sum(o, other).astype(BF16)
            send_sum(o, 0)
        for b in range(1, BLOCKS):
            for o in tp_far:
                send_sum(o, b)
        rs_acc[0] = partial_sum(0, other)
        for b, rows in enumerate(blocks):
            wait_for(
                rs_recv.at[n, pl.ds(0, n_tp - 1), pl.ds(0, BT)], sem_rs_r.at[n, b]
            )
            summed = rs_acc[0, rows, :]
            for o in range(1, n_tp):
                summed = summed + rs_recv[n, o - 1, rows, :].astype(F32)
            inverse = jnp.concatenate([inv_v[rows, :]] * (cols // HD), axis=1)
            vector = inverse * (gain_own * summed)

            @pl.when(n < SSTEP - 1)
            def _():
                xg[n + 1, tp, rows, :] = vector.astype(BF16)
                send_vector(n + 1, b)

            kry[n + 1, rows, :] = vector
            dif[n, rows, :] = kry[n, rows, :] - vector

        @pl.when(n < SSTEP - 1)
        def _():
            for b, rows in enumerate(blocks):
                send_grad_out(n + 1, b, rows)
            send_corr(n + 1)

        for a in range(SSTEP):

            @pl.when(n == a)
            def _():
                inner_rows(a)

        return carry

    lax.fori_loop(0, SSTEP, product, 0)

    square = jnp.concatenate(
        [tile[...], jnp.zeros((HD - tile.shape[0], HD), F32)], axis=0
    )
    whole = jnp.sum(square.T, axis=0, keepdims=True)
    start = 0
    for stage, devices in enumerate((stage_a, stage_b)):
        rows_out[stage] = whole
        for k, device in enumerate(devices):
            send(
                rows_out.at[stage],
                rows_in.at[start + k],
                sem_t_s,
                sem_t_r.at[stage],
                device,
            )
        wait_for(rows_in.at[pl.ds(start, len(devices))], sem_t_r.at[stage])
        whole = whole + jnp.sum(rows_in[start : start + len(devices)], axis=0)
        start += len(devices)
    spread = jnp.broadcast_to(whole, (HD, HD)).T

    def inner(a, b):
        place = pairs.index((a, b))
        return spread[place : place + 1]

    factor = {}
    for a in range(SSTEP):
        for b in range(a + 1):
            value = inner(a, b)
            for c in range(b):
                value = value - factor[a, c] * factor[b, c]
            factor[a, b] = jnp.sqrt(value) if a == b else value / factor[b, b]
    half = []
    for a in range(SSTEP):
        value = inner(a, None)
        for b in range(a):
            value = value - factor[a, b] * half[b]
        half.append(value / factor[a, a])
    coef = [None] * SSTEP
    for a in range(SSTEP - 1, -1, -1):
        value = half[a]
        for b in range(a + 1, SSTEP):
            value = value - factor[b, a] * coef[b]
        coef[a] = value / factor[a, a]
    coef = [jnp.concatenate([c] * (cols // HD), axis=1) for c in coef]
    adjoint = coef[0] * kry[0]
    for n in range(1, SSTEP):
        adjoint = adjoint + coef[n] * kry[n]
    adj_out[...] = adjoint
    residual = kry[0]
    for n in range(SSTEP):
        residual = residual - coef[n] * dif[n]
    res_out[...] = residual

    sent = 4 * REACH + 1
    wait_for(xs.at[pl.ds(0, n_tp - 1)], sem_xs_s)
    wait_for(win.at[:, pl.ds(0, sent * TOK)], sem_q_s)
    wait_for(att_own.at[0], sem_a_s)
    wait_for(stats.at[pl.ds(0, CHUNKS - 1)], sem_st_s)
    for n in range(SSTEP):
        wait_for(xg.at[n, pl.ds(0, n_tp - 1)], sem_xg_s.at[n])
        wait_for(g_win.at[n, pl.ds(0, sent * TOK)], sem_g_s.at[n])
        wait_for(c_win.at[n, pl.ds(0, sent)], sem_c_s.at[n])
        wait_for(g_swap.at[n], sem_sw_s.at[n])
        wait_for(rs_send.at[n], sem_rs_s.at[n])
    wait_for(rows_in, sem_t_s)


def on_device(sizes, state, cotangent, norm_gain, w_query, w_key, w_value, w_out):
    n_seq, n_tp, n_y, n_z = sizes
    tok, cols = state.shape
    width = n_tp * cols
    row_count = (2 * n_y - 1) + (n_z * n_tp - 1)
    dma = pltpu.SemaphoreType.DMA
    scratch = [
        pltpu.VMEM((width, 2 * HD), BF16),
        pltpu.VMEM((2, width, 2 * HD), BF16),
        pltpu.VMEM((2 * HD, width), BF16),
        pltpu.VMEM((1, width), F32),
        pltpu.VMEM((n_tp, tok, cols), BF16),
        pltpu.VMEM((tok, width), BF16),
        pltpu.VMEM((SSTEP, n_tp, tok, cols), BF16),
        pltpu.VMEM((2, 3, tok, HD), BF16),
        pltpu.VMEM((3, SPAN, HD), BF16),
        pltpu.VMEM((CHIP, HD), F32),
        pltpu.VMEM((2, tok, HD), F32),
        pltpu.VMEM((CHUNKS, 8, CHIP), F32),
        pltpu.VMEM((CHIP, SPAN), F32),
        pltpu.VMEM((CHIP, SPAN), F32),
        pltpu.VMEM((CHIP, SPAN), BF16),
        pltpu.VMEM((SSTEP, 2, tok, HD), BF16),
        pltpu.VMEM((SSTEP, SPAN, HD), BF16),
        pltpu.VMEM((SSTEP, 2, 1, HD), F32),
        pltpu.VMEM((SSTEP, 2 * CHUNKS, 1, HD), F32),
        pltpu.VMEM((SSTEP, 2, 3, tok, HD), BF16),
        pltpu.VMEM((SSTEP, 3, tok, HD), BF16),
        pltpu.VMEM((2, CHIP, HD), F32),
        pltpu.VMEM((n_tp, tok, cols), F32),
        pltpu.VMEM((SSTEP, n_tp - 1, tok, cols), BF16),
        pltpu.VMEM((SSTEP, n_tp - 1, tok, cols), BF16),
        pltpu.VMEM((SSTEP + 1, tok, cols), F32),
        pltpu.VMEM((SSTEP, tok, cols), F32),
        pltpu.VMEM((tok, HD), F32),
        pltpu.VMEM((16, HD), F32),
        pltpu.VMEM((2, 1, HD), F32),
        pltpu.VMEM((row_count, 1, HD), F32),
        dma((9,)),
        dma,
        dma((BLOCKS,)),
        dma((SSTEP,)),
        dma((SSTEP, BLOCKS)),
        dma,
        dma((CHUNKS, BLOCKS)),
        dma((CHUNKS,)),
        dma,
        dma,
        dma,
        dma,
        dma((SSTEP,)),
        dma((SSTEP, CHUNKS)),
        dma((SSTEP,)),
        dma((SSTEP, CHUNKS)),
        dma((SSTEP,)),
        dma((SSTEP, 2)),
        dma((SSTEP,)),
        dma((SSTEP, BLOCKS)),
        dma,
        dma((2,)),
    ]
    anywhere = pl.BlockSpec(memory_space=pl.ANY)
    return pl.pallas_call(
        functools.partial(kernel, sizes),
        out_shape=(pltpu.VMEM((tok, cols), F32), pltpu.VMEM((tok, cols), F32)),
        in_specs=[anywhere] * 7,
        out_specs=(pl.BlockSpec(memory_space=pltpu.VMEM),) * 2,
        scratch_shapes=scratch,
        compiler_params=pltpu.CompilerParams(
            collective_id=0, has_side_effects=True, vmem_limit_bytes=63 * 2**20
        ),
        name="block",
    )(state, cotangent, norm_gain.reshape(1, width), w_query, w_key, w_value, w_out)


def solution(mesh):
    n_seq, n_tp = mesh.shape["seq"], mesh.shape["tp"]
    n_chip = n_seq // 2
    n_y = 1
    while n_y * n_y < n_chip:
        n_y *= 2
    sizes = (n_seq, n_tp, n_y, n_chip // n_y)
    in_specs = (
        P("seq", "tp"),
        P("seq", "tp"),
        P(),
        P(None, "tp"),
        P(None, "tp"),
        P(None, "tp"),
        P("tp", None),
    )
    return jax.shard_map(
        functools.partial(on_device, sizes),
        mesh=mesh,
        in_specs=in_specs,
        out_specs=(P("seq", "tp"), P("seq", "tp")),
        check_vma=False,
    )
```

```python
import functools
import math

import jax
import jax.numpy as jnp
from jax import lax
from jax.experimental import pallas as pl
from jax.experimental.pallas import tpu as pltpu
from jax.sharding import PartitionSpec as P

HD = 128
HALF = 512
SSTEP = 4
EPSILON = 1e-05
TOK = 128
CHIP = 2 * TOK
SPAN = CHIP + 2 * HALF
REACH = HALF // CHIP
CHUNKS = 2 * REACH + 1
BLOCKS = 4
BT = TOK // BLOCKS
GRAD_BLOCKS = 4
GT = TOK // GRAD_BLOCKS
SCALE = 1.0 / math.sqrt(HD)
LOW = -1e30
MESH = pl.DeviceIdType.MESH
F32 = jnp.float32
BF16 = jnp.bfloat16

NT = (((1,), (1,)), ((), ()))
NN = (((1,), (0,)), ((), ()))


def dot(a, b, dims):
    return lax.dot_general(a, b, dims, preferred_element_type=F32)


def wait_for(ref, sem):
    pltpu.make_async_copy(ref, ref, sem).wait()


def kernel(
    sizes,
    state,
    cot,
    gain,
    w_query,
    w_key,
    w_value,
    w_out,
    adj_out,
    res_out,
    w_q,
    w_kv,
    w_o,
    gain_v,
    xs,
    normed_v,
    xg,
    qkv,
    win,
    att_head,
    att_own,
    stats,
    probs,
    probs_t,
    probs_tb,
    g_msg,
    g_win,
    c_msg,
    c_win,
    g_full,
    g_swap,
    kv_acc,
    rs_acc,
    rs_send,
    rs_recv,
    kry,
    dif,
    inv_v,
    tile,
    rows_out,
    rows_in,
    sem_load,
    sem_xs_s,
    sem_xs_r,
    sem_xg_s,
    sem_xg_r,
    sem_q_s,
    sem_kv_r,
    sem_q_r,
    sem_a_s,
    sem_a_r,
    sem_st_s,
    sem_st_r,
    sem_g_s,
    sem_g_r,
    sem_c_s,
    sem_c_r,
    sem_sw_s,
    sem_sw_r,
    sem_rs_s,
    sem_rs_r,
    sem_t_s,
    sem_t_r,
):
    n_seq, n_tp, n_y, n_z = sizes
    n_chip = n_seq // 2
    s = lax.axis_index("seq")
    tp = lax.axis_index("tp")
    chip = lax.div(s, 2)
    core = lax.rem(s, 2)
    y = lax.rem(chip, n_y)
    z = lax.div(chip, n_y)
    other = 1 - core
    cols = xs.shape[2]
    pair = (2 * chip + other, tp)

    def at_tp(offset):
        return lax.rem(tp + offset, n_tp)

    def at_chip(offset):
        return lax.rem(chip + offset + n_chip, n_chip)

    tp_far = sorted(range(1, n_tp), key=lambda o: -min(o, n_tp - o))
    near = (-1, 1)
    halo = [d for k in range(REACH, 0, -1) for d in (-k, k)]
    blocks = [slice(b * BT, (b + 1) * BT) for b in range(BLOCKS)]
    tp_device = {o: (s, at_tp(o)) for o in tp_far}
    toward = jnp.where(2 * y >= n_y, 1, -1)
    route = []
    for step in (*range(REACH, 0, -1), *range(-REACH, 0)):
        d = toward * step
        there = at_chip(d)
        devices = [(2 * there + h, tp) for h in range(2)]
        route.append((REACH - d, devices))
    beside = {d: (2 * at_chip(d) + core, tp) for d in halo}
    slot_start = {d: (2 * (REACH - d) + core) * TOK for d in (0, *halo)}
    tp_start = {o: at_tp(o) * cols for o in range(n_tp)}
    stage_a = [
        (2 * (z * n_y + lax.rem(y + oy, n_y)) + lax.rem(core + oc, 2), tp)
        for oy in range(n_y)
        for oc in range(2)
        if (oy, oc) != (0, 0)
    ]
    stage_b = [
        (2 * (lax.rem(z + oz, n_z) * n_y + y) + core, at_tp(ox))
        for oz in range(n_z)
        for ox in range(n_tp)
        if (oz, ox) != (0, 0)
    ]

    def send(src, dst, ssem, rsem, device):
        pltpu.make_async_remote_copy(
            src_ref=src,
            dst_ref=dst,
            send_sem=ssem,
            recv_sem=rsem,
            device_id=device,
            device_id_type=MESH,
        ).start()

    barrier = pltpu.get_barrier_semaphore()
    greeted = stage_b + stage_a
    for d in halo:
        for h in range(2):
            greeted.append((2 * at_chip(d) + h, tp))
    for device in greeted:
        pl.semaphore_signal(barrier, inc=1, device_id=device, device_id_type=MESH)

    loads = [
        (cot, kry.at[0]),
        (state, xs.at[tp]),
        (gain, gain_v),
    ]
    for h in range(2):
        for t, source in enumerate((w_key, w_value)):
            loads.append(
                (
                    source.at[:, pl.ds(h * HD, HD)],
                    w_kv.at[h, :, pl.ds(t * HD, HD)],
                )
            )
    loads += [(w_query, w_q), (w_out, w_o)]
    loading = [
        pltpu.make_async_copy(src, dst, sem_load.at[k])
        for k, (src, dst) in enumerate(loads)
    ]
    for copy in loading:
        copy.start()
    pl.semaphore_wait(barrier, len(greeted))

    for b in range(BLOCKS):
        for o in tp_far:
            send(
                state.at[pl.ds(b * BT, BT)],
                xs.at[tp, pl.ds(b * BT, BT)],
                sem_xs_s,
                sem_xs_r.at[b],
                tp_device[o],
            )

    def send_vector(n, b):
        for o in tp_far:
            send(
                xg.at[n, tp, pl.ds(b * BT, BT)],
                xg.at[n, tp, pl.ds(b * BT, BT)],
                sem_xg_s.at[n],
                sem_xg_r.at[n, b],
                tp_device[o],
            )

    def send_window(t, count, start, size, rsem):
        rows = pl.ds(start, size)
        place = pl.ds(t, count)

        def target(d):
            first = slot_start[d] + start
            return win.at[place, pl.ds(pl.multiple_of(first, BT), size)]

        send(qkv.at[other, place, rows], target(0), sem_q_s, rsem(REACH), pair)
        for d in near:
            for h in range(2):
                send(
                    qkv.at[h, place, rows],
                    target(d),
                    sem_q_s,
                    rsem(REACH - d),
                    (2 * at_chip(d) + h, tp),
                )
        own_rows = pl.ds(
            pl.multiple_of((2 * REACH + core) * TOK + start, BT), size
        )
        for k in range(t, t + count):
            win[k, own_rows, :] = qkv[core, k, start : start + size, :]

    def wait_kv(k, b):
        rows = BT if k == REACH else 2 * BT
        wait_for(win.at[pl.ds(1, 2), pl.ds(0, rows)], sem_kv_r.at[k, b])

    def wait_q(k):
        wait_for(win.at[0, pl.ds(0, TOK if k == REACH else CHIP)], sem_q_r.at[k])

    def pass_on(t, count, starts, size, rsem):
        for d in near:
            k = REACH - d
            for start in starts:
                first = k * CHIP + start
                send(
                    win.at[pl.ds(t, count), pl.ds(first, size)],
                    win.at[pl.ds(t, count), pl.ds(first - d * CHIP, size)],
                    sem_q_s,
                    rsem(k - d),
                    beside[d],
                )

    loading[2].wait()
    for b, rows in enumerate(blocks):
        wait_for(xs.at[pl.ds(0, n_tp - 1), pl.ds(0, BT)], sem_xs_r.at[b])
        if b == 0:
            loading[0].wait()
            loading[1].wait()
        if b == BLOCKS - 1:
            xg[0, tp] = kry[0].astype(BF16)
            for c in range(BLOCKS):
                send_vector(0, c)
        total = jnp.zeros((BT, 1), F32)
        for r in range(n_tp):
            block = xs[r, rows, :].astype(F32)
            total = total + jnp.sum(block * block, axis=1, keepdims=True)
        inverse = lax.rsqrt(total * (1.0 / (n_tp * cols)) + EPSILON)
        inv_v[rows, :] = jnp.broadcast_to(inverse, (BT, HD))
        normed = jnp.concatenate(
            [
                (
                    xs[r, rows, :].astype(F32)
                    * inverse
                    * gain_v[:, r * cols : (r + 1) * cols]
                ).astype(BF16)
                for r in range(n_tp)
            ],
            axis=1,
        )
        normed_v[rows, :] = normed
        for h in range(2):
            if b == 0:
                loading[3 + 2 * h].wait()
                loading[4 + 2 * h].wait()
            acc = dot(normed, w_kv[h], NN).astype(BF16)
            for t in range(2):
                qkv[h, 1 + t, rows, :] = acc[:, t * HD : (t + 1) * HD]
        send_window(1, 2, b * BT, BT, lambda k, b=b: sem_kv_r.at[k, b])
    loading[7].wait()
    acc = dot(normed_v[...], w_q[...], NN).astype(BF16)
    for h in range(2):
        qkv[h, 0] = acc[:, h * HD : (h + 1) * HD]
    send_window(0, 1, 0, TOK, lambda k: sem_q_r.at[k])
    for b in range(BLOCKS):
        for d in near:
            wait_kv(REACH - d, b)
        pass_on(1, 2, [b * BT, TOK + b * BT], BT, lambda k, b=b: sem_kv_r.at[k, b])

    def send_grad_out(n, b):
        rows = slice(b * GT, (b + 1) * GT)
        for c in range(BLOCKS):
            if b * GT <= c * BT < (b + 1) * GT:
                wait_for(xg.at[n, pl.ds(0, n_tp - 1), pl.ds(0, BT)], sem_xg_r.at[n, c])
        acc = jnp.zeros((GT, 2 * HD), F32)
        for r in range(n_tp):
            acc = acc + dot(xg[n, r, rows, :], w_o[:, r * cols : (r + 1) * cols], NT)
        acc = acc.astype(BF16)
        for h in range(2):
            g_msg[n, h, rows, :] = acc[:, h * HD : (h + 1) * HD]
        taken = pl.ds(b * GT, GT)

        def target(k):
            first = (2 * k + core) * TOK + b * GT
            return pl.ds(pl.multiple_of(first, GT), GT)

        send(
            g_msg.at[n, other, taken],
            g_win.at[n, target(REACH)],
            sem_g_s.at[n],
            sem_g_r.at[n, REACH],
            pair,
        )
        for k, devices in route:
            for h in range(2):
                send(
                    g_msg.at[n, h, taken],
                    g_win.at[n, target(k)],
                    sem_g_s.at[n],
                    sem_g_r.at[n, k],
                    devices[h],
                )
        g_win[n, target(REACH), :] = g_msg[n, core, rows, :]

    def send_corr(n):
        for h in range(2):
            c_msg[n, h] = jnp.sum(
                (g_msg[n, h].astype(F32) * att_own[h]).T, axis=0, keepdims=True
            )
        send(
            c_msg.at[n, other],
            c_win.at[n, 2 * REACH + core],
            sem_c_s.at[n],
            sem_c_r.at[n, REACH],
            pair,
        )
        for k, devices in route:
            for h in range(2):
                send(
                    c_msg.at[n, h],
                    c_win.at[n, 2 * k + core],
                    sem_c_s.at[n],
                    sem_c_r.at[n, k],
                    devices[h],
                )
        c_win[n, 2 * REACH + core] = c_msg[n, core]

    arrival = sorted(range(CHUNKS), key=lambda k: abs(k - REACH))
    own = slice(HALF, HALF + CHIP)

    def valid(k):
        row = lax.broadcasted_iota(jnp.int32, (CHIP, CHIP), 0)
        col = lax.broadcasted_iota(jnp.int32, (CHIP, CHIP), 1) + k * CHIP
        place = chip * CHIP - HALF + col
        away = row + HALF - col
        return (
            (away <= HALF)
            & (away >= -HALF)
            & (place >= 0)
            & (place < n_chip * CHIP)
        )

    def part(k):
        return slice(k * CHIP, (k + 1) * CHIP)

    def span(k):
        return pl.ds(pl.multiple_of(k * CHIP, CHIP), CHIP)

    soon = [REACH, *(REACH - toward * step for step in range(1, REACH + 1))]
    last = [REACH + toward * step for step in range(1, REACH + 1)]

    def scores_of(k, peak):
        scores = dot(win[0, own, :], win[1, part(k), :], NT) * SCALE
        scores = jnp.where(valid(k), scores, LOW)
        probs[:, part(k)] = scores
        return jnp.maximum(peak, jnp.max(scores, axis=1, keepdims=True))

    wait_q(REACH)
    for b in range(BLOCKS):
        wait_kv(REACH, b)
    peak = jnp.full((CHIP, 1), LOW, F32)
    for k in arrival[:3]:
        peak = scores_of(k, peak)
    for d in near:
        wait_q(REACH - d)
    pass_on(0, 1, [0], CHIP, lambda k: sem_q_r.at[k])
    loading[8].wait()
    for b in range(GRAD_BLOCKS):
        send_grad_out(0, b)
    for k in arrival[3:]:
        for b in range(BLOCKS):
            wait_kv(k, b)
        peak = scores_of(k, peak)
    mass = jnp.zeros((CHIP, 1), F32)
    for k in arrival:
        raw = jnp.exp(probs[:, part(k)] - peak)
        probs[:, part(k)] = raw
        mass = mass + jnp.sum(raw, axis=1, keepdims=True)
    share = 1.0 / mass
    both = jnp.concatenate(
        [
            jnp.broadcast_to(peak, (CHIP, HD)).T[0:1],
            jnp.broadcast_to(share, (CHIP, HD)).T[0:1],
            jnp.zeros((6, CHIP), F32),
        ],
        axis=0,
    )
    stats[REACH] = both
    for d in halo:
        send(
            stats.at[REACH],
            stats.at[REACH - d],
            sem_st_s,
            sem_st_r,
            beside[d],
        )
    attended = jnp.zeros((CHIP, HD), F32)
    for k in arrival:
        weights = probs[:, part(k)] * share
        probs[:, part(k)] = weights * SCALE
        attended = attended + dot(weights.astype(BF16), win[2, part(k), :], NN)
    att_head[...] = attended
    other_half = pl.ds(pl.multiple_of(other * TOK, TOK), TOK)
    own_half = pl.ds(pl.multiple_of(core * TOK, TOK), TOK)
    send(att_head.at[other_half], att_own.at[core], sem_a_s, sem_a_r, pair)
    att_own[core] = att_head[own_half, :]
    wait_for(att_own.at[0], sem_a_r)
    send_corr(0)

    keys = win[1, own, :]
    wait_for(stats.at[pl.ds(0, CHUNKS - 1)], sem_st_r)
    for k in arrival:
        if abs(k - REACH) == 2:
            wait_q(k)
        scores = dot(keys, win[0, part(k), :], NT) * SCALE
        pair_stats = stats[k]
        scores = jnp.where(valid(k), scores - pair_stats[0:1], LOW)
        weights = jnp.exp(scores) * pair_stats[1:2]
        probs_t[:, part(k)] = weights * SCALE
        probs_tb[:, part(k)] = weights.astype(BF16)

    gain_own = gain_v[:, pl.ds(pl.multiple_of(tp * cols, cols), cols)]

    def inner_row(a, b):
        row = jnp.sum(dif[a] * (kry[0] if b is None else dif[b]), axis=0, keepdims=True)
        folded = row[:, 0:HD]
        for start in range(HD, cols, HD):
            folded = folded + row[:, start : start + HD]
        return folded

    pairs = [(a, b) for a in range(SSTEP) for b in list(range(a + 1)) + [None]]

    def inner_rows(a):
        for place, (first, second) in enumerate(pairs):
            if first == a:
                tile[place : place + 1, :] = inner_row(first, second)

    tile[...] = jnp.zeros(tile.shape, F32)

    def product(n, carry):
        def give_back(t, whole):
            whole = whole.astype(BF16)
            first, second = whole[0:TOK], whole[TOK:CHIP]
            mine = core == 0
            g_full[n, core, t] = jnp.where(mine, first, second)
            g_swap[n, t] = jnp.where(mine, second, first)

        def both_heads(t):
            return jnp.concatenate([g_full[n, 0, t], g_full[n, 1, t]], axis=1)

        def tp_rows(o):
            return pl.ds(pl.multiple_of(tp_start[o], cols), cols)

        wait_for(g_win.at[n, pl.ds(0, TOK)], sem_g_r.at[n, REACH])
        grad = g_win[n, own, :]
        corr = jnp.sum(grad.astype(F32) * att_head[...], axis=1, keepdims=True)
        grad_q = jnp.zeros((CHIP, HD), F32)
        for k in range(CHUNKS):
            grad_p = dot(grad, win[2, part(k), :], NT)
            score = (probs[:, part(k)] * (grad_p - corr)).astype(BF16)
            grad_q = grad_q + dot(score, win[1, part(k), :], NN)
        give_back(0, grad_q)
        send(
            g_swap.at[n, pl.ds(0, 1)],
            g_full.at[n, core, pl.ds(0, 1)],
            sem_sw_s.at[n],
            sem_sw_r.at[n, 0],
            pair,
        )
        def key_side(k, values, wide, low):
            grad = g_win[n, span(k), :]
            corr = jnp.concatenate([c_win[n, 2 * k], c_win[n, 2 * k + 1]], axis=1)
            score = (wide * (dot(values, grad, NT) - corr)).astype(BF16)
            return dot(score, win[0, span(k), :], NN), dot(low, grad, NN)

        def wait_grad(k):
            mine = k is REACH
            if not mine:
                wait_for(g_win.at[n, pl.ds(0, CHIP)], sem_g_r.at[n, k])
            wait_for(c_win.at[n, pl.ds(0, 1 if mine else 2)], sem_c_r.at[n, k])

        for place, k in enumerate(soon):
            wait_grad(k)
            grad_k, grad_v = key_side(
                k, win[2, own, :], probs_t[:, span(k)], probs_tb[:, span(k)]
            )
            if place == 0:
                kv_acc[0] = grad_k
                kv_acc[1] = grad_v
                wait_for(g_swap.at[n, pl.ds(0, 1)], sem_sw_r.at[n, 0])
                for o in range(n_tp):
                    rs_acc[o] = dot(both_heads(0), w_q[tp_rows(o), :], NT)
            else:
                kv_acc[0] += grad_k
                kv_acc[1] += grad_v
        for k in last:
            wait_grad(k)
        for token_core in (other, core):
            taken = pl.ds(pl.multiple_of(token_core * TOK, TOK), TOK)
            window = pl.ds(pl.multiple_of(HALF + token_core * TOK, TOK), TOK)
            sums = [kv_acc[0, taken, :], kv_acc[1, taken, :]]
            for k in last:
                grad_k, grad_v = key_side(
                    k,
                    win[2, window, :],
                    probs_t[taken, span(k)],
                    probs_tb[taken, span(k)],
                )
                sums = [sums[0] + grad_k, sums[1] + grad_v]
            for t in range(2):
                if token_core is other:
                    g_swap[n, 1 + t] = sums[t].astype(BF16)
                else:
                    g_full[n, core, 1 + t] = sums[t].astype(BF16)
            if token_core is other:
                send(
                    g_swap.at[n, pl.ds(1, 2)],
                    g_full.at[n, core, pl.ds(1, 2)],
                    sem_sw_s.at[n],
                    sem_sw_r.at[n, 1],
                    pair,
                )

        def partial_sum(o, head):
            late = jnp.concatenate([g_full[n, head, 1], g_full[n, head, 2]], axis=1)
            return rs_acc[o] + dot(late, w_kv[head, tp_rows(o), :], NT)

        for o in range(n_tp):
            rs_acc[o] = partial_sum(o, core)
        wait_for(g_swap.at[n, pl.ds(1, 2)], sem_sw_r.at[n, 1])

        def send_sum(o, b):
            send(
                rs_send.at[n, o - 1, pl.ds(b * BT, BT)],
                rs_recv.at[n, o - 1, pl.ds(b * BT, BT)],
                sem_rs_s.at[n],
                sem_rs_r.at[n, b],
                tp_device[o],
            )

        for o in tp_far:
            rs_send[n, o - 1] = partial_sum(o, other).astype(BF16)
            send_sum(o, 0)
        for b in range(1, BLOCKS):
            for o in tp_far:
                send_sum(o, b)
        rs_acc[0] = partial_sum(0, other)
        for b, rows in enumerate(blocks):
            wait_for(
                rs_recv.at[n, pl.ds(0, n_tp - 1), pl.ds(0, BT)], sem_rs_r.at[n, b]
            )
            summed = rs_acc[0, rows, :]
            for o in range(1, n_tp):
                summed = summed + rs_recv[n, o - 1, rows, :].astype(F32)
            inverse = jnp.concatenate([inv_v[rows, :]] * (cols // HD), axis=1)
            vector = inverse * (gain_own * summed)

            @pl.when(n < SSTEP - 1)
            def _():
                xg[n + 1, tp, rows, :] = vector.astype(BF16)
                send_vector(n + 1, b)

            kry[n + 1, rows, :] = vector
            dif[n, rows, :] = kry[n, rows, :] - vector

        @pl.when(n < SSTEP - 1)
        def _():
            for b in range(GRAD_BLOCKS):
                send_grad_out(n + 1, b)
            send_corr(n + 1)

        for a in range(SSTEP):

            @pl.when(n == a)
            def _():
                inner_rows(a)

        return carry

    lax.fori_loop(0, SSTEP, product, 0)

    square = jnp.concatenate(
        [tile[...], jnp.zeros((HD - tile.shape[0], HD), F32)], axis=0
    )
    whole = jnp.sum(square.T, axis=0, keepdims=True)
    start = 0
    for stage, devices in enumerate((stage_a, stage_b)):
        rows_out[stage] = whole
        for k, device in enumerate(devices):
            send(
                rows_out.at[stage],
                rows_in.at[start + k],
                sem_t_s,
                sem_t_r.at[stage],
                device,
            )
        wait_for(rows_in.at[pl.ds(start, len(devices))], sem_t_r.at[stage])
        whole = whole + jnp.sum(rows_in[start : start + len(devices)], axis=0)
        start += len(devices)
    spread = jnp.broadcast_to(whole, (HD, HD)).T

    def inner(a, b):
        place = pairs.index((a, b))
        return spread[place : place + 1]

    factor = {}
    for a in range(SSTEP):
        for b in range(a + 1):
            value = inner(a, b)
            for c in range(b):
                value = value - factor[a, c] * factor[b, c]
            factor[a, b] = jnp.sqrt(value) if a == b else value / factor[b, b]
    half = []
    for a in range(SSTEP):
        value = inner(a, None)
        for b in range(a):
            value = value - factor[a, b] * half[b]
        half.append(value / factor[a, a])
    coef = [None] * SSTEP
    for a in range(SSTEP - 1, -1, -1):
        value = half[a]
        for b in range(a + 1, SSTEP):
            value = value - factor[b, a] * coef[b]
        coef[a] = value / factor[a, a]
    coef = [jnp.concatenate([c] * (cols // HD), axis=1) for c in coef]
    adjoint = coef[0] * kry[0]
    for n in range(1, SSTEP):
        adjoint = adjoint + coef[n] * kry[n]
    adj_out[...] = adjoint
    residual = kry[0]
    for n in range(SSTEP):
        residual = residual - coef[n] * dif[n]
    res_out[...] = residual

    sent = 4 * REACH + 1
    wait_for(xs.at[pl.ds(0, n_tp - 1)], sem_xs_s)
    wait_for(win.at[:, pl.ds(0, sent * TOK)], sem_q_s)
    wait_for(att_own.at[0], sem_a_s)
    wait_for(stats.at[pl.ds(0, CHUNKS - 1)], sem_st_s)
    for n in range(SSTEP):
        wait_for(xg.at[n, pl.ds(0, n_tp - 1)], sem_xg_s.at[n])
        wait_for(g_win.at[n, pl.ds(0, sent * TOK)], sem_g_s.at[n])
        wait_for(c_win.at[n, pl.ds(0, sent)], sem_c_s.at[n])
        wait_for(g_swap.at[n], sem_sw_s.at[n])
        wait_for(rs_send.at[n], sem_rs_s.at[n])
    wait_for(rows_in, sem_t_s)


def on_device(sizes, state, cotangent, norm_gain, w_query, w_key, w_value, w_out):
    n_seq, n_tp, n_y, n_z = sizes
    tok, cols = state.shape
    width = n_tp * cols
    row_count = (2 * n_y - 1) + (n_z * n_tp - 1)
    dma = pltpu.SemaphoreType.DMA
    scratch = [
        pltpu.VMEM((width, 2 * HD), BF16),
        pltpu.VMEM((2, width, 2 * HD), BF16),
        pltpu.VMEM((2 * HD, width), BF16),
        pltpu.VMEM((1, width), F32),
        pltpu.VMEM((n_tp, tok, cols), BF16),
        pltpu.VMEM((tok, width), BF16),
        pltpu.VMEM((SSTEP, n_tp, tok, cols), BF16),
        pltpu.VMEM((2, 3, tok, HD), BF16),
        pltpu.VMEM((3, SPAN, HD), BF16),
        pltpu.VMEM((CHIP, HD), F32),
        pltpu.VMEM((2, tok, HD), F32),
        pltpu.VMEM((CHUNKS, 8, CHIP), F32),
        pltpu.VMEM((CHIP, SPAN), F32),
        pltpu.VMEM((CHIP, SPAN), F32),
        pltpu.VMEM((CHIP, SPAN), BF16),
        pltpu.VMEM((SSTEP, 2, tok, HD), BF16),
        pltpu.VMEM((SSTEP, SPAN, HD), BF16),
        pltpu.VMEM((SSTEP, 2, 1, HD), F32),
        pltpu.VMEM((SSTEP, 2 * CHUNKS, 1, HD), F32),
        pltpu.VMEM((SSTEP, 2, 3, tok, HD), BF16),
        pltpu.VMEM((SSTEP, 3, tok, HD), BF16),
        pltpu.VMEM((2, CHIP, HD), F32),
        pltpu.VMEM((n_tp, tok, cols), F32),
        pltpu.VMEM((SSTEP, n_tp - 1, tok, cols), BF16),
        pltpu.VMEM((SSTEP, n_tp - 1, tok, cols), BF16),
        pltpu.VMEM((SSTEP + 1, tok, cols), F32),
        pltpu.VMEM((SSTEP, tok, cols), F32),
        pltpu.VMEM((tok, HD), F32),
        pltpu.VMEM((16, HD), F32),
        pltpu.VMEM((2, 1, HD), F32),
        pltpu.VMEM((row_count, 1, HD), F32),
        dma((9,)),
        dma,
        dma((BLOCKS,)),
        dma((SSTEP,)),
        dma((SSTEP, BLOCKS)),
        dma,
        dma((CHUNKS, BLOCKS)),
        dma((CHUNKS,)),
        dma,
        dma,
        dma,
        dma,
        dma((SSTEP,)),
        dma((SSTEP, CHUNKS)),
        dma((SSTEP,)),
        dma((SSTEP, CHUNKS)),
        dma((SSTEP,)),
        dma((SSTEP, 2)),
        dma((SSTEP,)),
        dma((SSTEP, BLOCKS)),
        dma,
        dma((2,)),
    ]
    anywhere = pl.BlockSpec(memory_space=pl.ANY)
    return pl.pallas_call(
        functools.partial(kernel, sizes),
        out_shape=(pltpu.VMEM((tok, cols), F32), pltpu.VMEM((tok, cols), F32)),
        in_specs=[anywhere] * 7,
        out_specs=(pl.BlockSpec(memory_space=pltpu.VMEM),) * 2,
        scratch_shapes=scratch,
        compiler_params=pltpu.CompilerParams(
            collective_id=0, has_side_effects=True, vmem_limit_bytes=63 * 2**20
        ),
        name="block",
    )(state, cotangent, norm_gain.reshape(1, width), w_query, w_key, w_value, w_out)


def solution(mesh):
    n_seq, n_tp = mesh.shape["seq"], mesh.shape["tp"]
    n_chip = n_seq // 2
    n_y = 1
    while n_y * n_y < n_chip:
        n_y *= 2
    sizes = (n_seq, n_tp, n_y, n_chip // n_y)
    in_specs = (
        P("seq", "tp"),
        P("seq", "tp"),
        P(),
        P(None, "tp"),
        P(None, "tp"),
        P(None, "tp"),
        P("tp", None),
    )
    return jax.shard_map(
        functools.partial(on_device, sizes),
        mesh=mesh,
        in_specs=in_specs,
        out_specs=(P("seq", "tp"), P("seq", "tp")),
        check_vma=False,
    )
```

```python
import functools
import math

import jax
import jax.numpy as jnp
from jax import lax
from jax.experimental import pallas as pl
from jax.experimental.pallas import tpu as pltpu
from jax.sharding import PartitionSpec as P

HD = 128
HALF = 512
SSTEP = 4
EPSILON = 1e-05
TOK = 128
CHIP = 2 * TOK
SPAN = CHIP + 2 * HALF
REACH = HALF // CHIP
CHUNKS = 2 * REACH + 1
BLOCKS = 4
BT = TOK // BLOCKS
GRAD_BLOCKS = 4
GT = TOK // GRAD_BLOCKS
SCALE = 1.0 / math.sqrt(HD)
LOW = -1e30
MESH = pl.DeviceIdType.MESH
F32 = jnp.float32
BF16 = jnp.bfloat16

NT = (((1,), (1,)), ((), ()))
NN = (((1,), (0,)), ((), ()))


def dot(a, b, dims):
    return lax.dot_general(a, b, dims, preferred_element_type=F32)


def wait_for(ref, sem):
    pltpu.make_async_copy(ref, ref, sem).wait()


def kernel(
    sizes,
    state,
    cot,
    gain,
    w_query,
    w_key,
    w_value,
    w_out,
    adj_out,
    res_out,
    w_q,
    w_kv,
    w_o,
    gain_v,
    xs,
    normed_v,
    xg,
    qkv,
    win,
    att_head,
    att_own,
    stats,
    probs,
    probs_t,
    probs_tb,
    g_msg,
    g_win,
    c_msg,
    c_win,
    g_full,
    g_swap,
    kv_acc,
    rs_acc,
    rs_send,
    rs_recv,
    kry,
    dif,
    inv_v,
    tile,
    rows_out,
    rows_in,
    sem_load,
    sem_xs_s,
    sem_xs_r,
    sem_xg_s,
    sem_xg_r,
    sem_q_s,
    sem_kv_r,
    sem_q_r,
    sem_a_s,
    sem_a_r,
    sem_st_s,
    sem_st_r,
    sem_g_s,
    sem_g_r,
    sem_c_s,
    sem_c_r,
    sem_sw_s,
    sem_sw_r,
    sem_rs_s,
    sem_rs_r,
    sem_t_s,
    sem_t_r,
):
    n_seq, n_tp, n_y, n_z = sizes
    n_chip = n_seq // 2
    s = lax.axis_index("seq")
    tp = lax.axis_index("tp")
    chip = lax.div(s, 2)
    core = lax.rem(s, 2)
    y = lax.rem(chip, n_y)
    z = lax.div(chip, n_y)
    other = 1 - core
    cols = xs.shape[2]
    pair = (2 * chip + other, tp)

    def at_tp(offset):
        return lax.rem(tp + offset, n_tp)

    def at_chip(offset):
        return lax.rem(chip + offset + n_chip, n_chip)

    tp_far = sorted(range(1, n_tp), key=lambda o: -min(o, n_tp - o))
    near = (-1, 1)
    halo = [d for k in range(REACH, 0, -1) for d in (-k, k)]
    blocks = [slice(b * BT, (b + 1) * BT) for b in range(BLOCKS)]
    tp_device = {o: (s, at_tp(o)) for o in tp_far}
    toward = jnp.where(2 * y >= n_y, 1, -1)
    route = []
    for step in (*range(REACH, 0, -1), *range(-REACH, 0)):
        d = toward * step
        there = at_chip(d)
        devices = [(2 * there + h, tp) for h in range(2)]
        route.append((REACH - d, devices))
    beside = {d: (2 * at_chip(d) + core, tp) for d in halo}
    slot_start = {d: (2 * (REACH - d) + core) * TOK for d in (0, *halo)}
    tp_start = {o: at_tp(o) * cols for o in range(n_tp)}
    stage_a = [
        (2 * (z * n_y + lax.rem(y + oy, n_y)) + lax.rem(core + oc, 2), tp)
        for oy in range(n_y)
        for oc in range(2)
        if (oy, oc) != (0, 0)
    ]
    stage_b = [
        (2 * (lax.rem(z + oz, n_z) * n_y + y) + core, at_tp(ox))
        for oz in range(n_z)
        for ox in range(n_tp)
        if (oz, ox) != (0, 0)
    ]

    def send(src, dst, ssem, rsem, device):
        pltpu.make_async_remote_copy(
            src_ref=src,
            dst_ref=dst,
            send_sem=ssem,
            recv_sem=rsem,
            device_id=device,
            device_id_type=MESH,
        ).start()

    barrier = pltpu.get_barrier_semaphore()
    greeted = stage_b + stage_a
    for d in halo:
        for h in range(2):
            greeted.append((2 * at_chip(d) + h, tp))
    for device in greeted:
        pl.semaphore_signal(barrier, inc=1, device_id=device, device_id_type=MESH)

    loads = [
        (cot, kry.at[0]),
        (state, xs.at[tp]),
        (gain, gain_v),
    ]
    for h in range(2):
        for t, source in enumerate((w_key, w_value)):
            loads.append(
                (
                    source.at[:, pl.ds(h * HD, HD)],
                    w_kv.at[h, :, pl.ds(t * HD, HD)],
                )
            )
    loads += [(w_query, w_q), (w_out, w_o)]
    loading = [
        pltpu.make_async_copy(src, dst, sem_load.at[k])
        for k, (src, dst) in enumerate(loads)
    ]
    for copy in loading:
        copy.start()
    pl.semaphore_wait(barrier, len(greeted))

    for b in range(BLOCKS):
        for o in tp_far:
            send(
                state.at[pl.ds(b * BT, BT)],
                xs.at[tp, pl.ds(b * BT, BT)],
                sem_xs_s,
                sem_xs_r.at[b],
                tp_device[o],
            )

    def send_vector(n, b):
        for o in tp_far:
            send(
                xg.at[n, tp, pl.ds(b * BT, BT)],
                xg.at[n, tp, pl.ds(b * BT, BT)],
                sem_xg_s.at[n],
                sem_xg_r.at[n, b],
                tp_device[o],
            )

    def send_window(t, count, start, size, rsem):
        rows = pl.ds(start, size)
        place = pl.ds(t, count)

        def target(d):
            first = slot_start[d] + start
            return win.at[place, pl.ds(pl.multiple_of(first, BT), size)]

        send(qkv.at[other, place, rows], target(0), sem_q_s, rsem(REACH), pair)
        for d in near:
            for h in range(2):
                send(
                    qkv.at[h, place, rows],
                    target(d),
                    sem_q_s,
                    rsem(REACH - d),
                    (2 * at_chip(d) + h, tp),
                )
        own_rows = pl.ds(
            pl.multiple_of((2 * REACH + core) * TOK + start, BT), size
        )
        for k in range(t, t + count):
            win[k, own_rows, :] = qkv[core, k, start : start + size, :]

    def wait_kv(k, b):
        rows = BT if k == REACH else 2 * BT
        wait_for(win.at[pl.ds(1, 2), pl.ds(0, rows)], sem_kv_r.at[k, b])

    def wait_q(k):
        wait_for(win.at[0, pl.ds(0, TOK if k == REACH else CHIP)], sem_q_r.at[k])

    def pass_on(t, count, starts, size, rsem):
        for d in near:
            k = REACH - d
            for start in starts:
                first = k * CHIP + start
                send(
                    win.at[pl.ds(t, count), pl.ds(first, size)],
                    win.at[pl.ds(t, count), pl.ds(first - d * CHIP, size)],
                    sem_q_s,
                    rsem(k - d),
                    beside[d],
                )

    loading[2].wait()
    for b, rows in enumerate(blocks):
        wait_for(xs.at[pl.ds(0, n_tp - 1), pl.ds(0, BT)], sem_xs_r.at[b])
        if b == 0:
            loading[0].wait()
            loading[1].wait()
        if b == 0:
            xg[0, tp] = kry[0].astype(BF16)
            for c in range(BLOCKS):
                send_vector(0, c)
        total = jnp.zeros((BT, 1), F32)
        for r in range(n_tp):
            block = xs[r, rows, :].astype(F32)
            total = total + jnp.sum(block * block, axis=1, keepdims=True)
        inverse = lax.rsqrt(total * (1.0 / (n_tp * cols)) + EPSILON)
        inv_v[rows, :] = jnp.broadcast_to(inverse, (BT, HD))
        normed = jnp.concatenate(
            [
                (
                    xs[r, rows, :].astype(F32)
                    * inverse
                    * gain_v[:, r * cols : (r + 1) * cols]
                ).astype(BF16)
                for r in range(n_tp)
            ],
            axis=1,
        )
        normed_v[rows, :] = normed
        for h in range(2):
            if b == 0:
                loading[3 + 2 * h].wait()
                loading[4 + 2 * h].wait()
            acc = dot(normed, w_kv[h], NN).astype(BF16)
            for t in range(2):
                qkv[h, 1 + t, rows, :] = acc[:, t * HD : (t + 1) * HD]
        send_window(1, 2, b * BT, BT, lambda k, b=b: sem_kv_r.at[k, b])
    loading[7].wait()
    acc = dot(normed_v[...], w_q[...], NN).astype(BF16)
    for h in range(2):
        qkv[h, 0] = acc[:, h * HD : (h + 1) * HD]
    send_window(0, 1, 0, TOK, lambda k: sem_q_r.at[k])
    for b in range(BLOCKS):
        for d in near:
            wait_kv(REACH - d, b)
        pass_on(1, 2, [b * BT, TOK + b * BT], BT, lambda k, b=b: sem_kv_r.at[k, b])

    def send_grad_out(n, b):
        rows = slice(b * GT, (b + 1) * GT)
        for c in range(BLOCKS):
            if b * GT <= c * BT < (b + 1) * GT:
                wait_for(xg.at[n, pl.ds(0, n_tp - 1), pl.ds(0, BT)], sem_xg_r.at[n, c])
        acc = jnp.zeros((GT, 2 * HD), F32)
        for r in range(n_tp):
            acc = acc + dot(xg[n, r, rows, :], w_o[:, r * cols : (r + 1) * cols], NT)
        acc = acc.astype(BF16)
        for h in range(2):
            g_msg[n, h, rows, :] = acc[:, h * HD : (h + 1) * HD]
        taken = pl.ds(b * GT, GT)

        def target(k):
            first = (2 * k + core) * TOK + b * GT
            return pl.ds(pl.multiple_of(first, GT), GT)

        send(
            g_msg.at[n, other, taken],
            g_win.at[n, target(REACH)],
            sem_g_s.at[n],
            sem_g_r.at[n, REACH],
            pair,
        )
        for k, devices in route:
            for h in range(2):
                send(
                    g_msg.at[n, h, taken],
                    g_win.at[n, target(k)],
                    sem_g_s.at[n],
                    sem_g_r.at[n, k],
                    devices[h],
                )
        g_win[n, target(REACH), :] = g_msg[n, core, rows, :]

    def send_corr(n):
        for h in range(2):
            c_msg[n, h] = jnp.sum(
                (g_msg[n, h].astype(F32) * att_own[h]).T, axis=0, keepdims=True
            )
        send(
            c_msg.at[n, other],
            c_win.at[n, 2 * REACH + core],
            sem_c_s.at[n],
            sem_c_r.at[n, REACH],
            pair,
        )
        for k, devices in route:
            for h in range(2):
                send(
                    c_msg.at[n, h],
                    c_win.at[n, 2 * k + core],
                    sem_c_s.at[n],
                    sem_c_r.at[n, k],
                    devices[h],
                )
        c_win[n, 2 * REACH + core] = c_msg[n, core]

    arrival = sorted(range(CHUNKS), key=lambda k: abs(k - REACH))
    own = slice(HALF, HALF + CHIP)

    def valid(k):
        row = lax.broadcasted_iota(jnp.int32, (CHIP, CHIP), 0)
        col = lax.broadcasted_iota(jnp.int32, (CHIP, CHIP), 1) + k * CHIP
        place = chip * CHIP - HALF + col
        away = row + HALF - col
        return (
            (away <= HALF)
            & (away >= -HALF)
            & (place >= 0)
            & (place < n_chip * CHIP)
        )

    def part(k):
        return slice(k * CHIP, (k + 1) * CHIP)

    def span(k):
        return pl.ds(pl.multiple_of(k * CHIP, CHIP), CHIP)

    soon = [REACH, *(REACH - toward * step for step in range(1, REACH + 1))]
    last = [REACH + toward * step for step in range(1, REACH + 1)]

    def scores_of(k, peak):
        scores = dot(win[0, own, :], win[1, part(k), :], NT) * SCALE
        scores = jnp.where(valid(k), scores, LOW)
        probs[:, part(k)] = scores
        return jnp.maximum(peak, jnp.max(scores, axis=1, keepdims=True))

    wait_q(REACH)
    for b in range(BLOCKS):
        wait_kv(REACH, b)
    peak = jnp.full((CHIP, 1), LOW, F32)
    for k in arrival[:3]:
        peak = scores_of(k, peak)
    loading[8].wait()
    for b in range(GRAD_BLOCKS):
        send_grad_out(0, b)
    for d in near:
        wait_q(REACH - d)
    pass_on(0, 1, [0], CHIP, lambda k: sem_q_r.at[k])
    for k in arrival[3:]:
        for b in range(BLOCKS):
            wait_kv(k, b)
        peak = scores_of(k, peak)
    mass = jnp.zeros((CHIP, 1), F32)
    for k in arrival:
        raw = jnp.exp(probs[:, part(k)] - peak)
        probs[:, part(k)] = raw
        mass = mass + jnp.sum(raw, axis=1, keepdims=True)
    share = 1.0 / mass
    both = jnp.concatenate(
        [
            jnp.broadcast_to(peak, (CHIP, HD)).T[0:1],
            jnp.broadcast_to(share, (CHIP, HD)).T[0:1],
            jnp.zeros((6, CHIP), F32),
        ],
        axis=0,
    )
    stats[REACH] = both
    for d in halo:
        send(
            stats.at[REACH],
            stats.at[REACH - d],
            sem_st_s,
            sem_st_r,
            beside[d],
        )
    attended = jnp.zeros((CHIP, HD), F32)
    for k in arrival:
        weights = probs[:, part(k)] * share
        probs[:, part(k)] = weights * SCALE
        attended = attended + dot(weights.astype(BF16), win[2, part(k), :], NN)
    att_head[...] = attended
    other_half = pl.ds(pl.multiple_of(other * TOK, TOK), TOK)
    own_half = pl.ds(pl.multiple_of(core * TOK, TOK), TOK)
    send(att_head.at[other_half], att_own.at[core], sem_a_s, sem_a_r, pair)
    att_own[core] = att_head[own_half, :]
    wait_for(att_own.at[0], sem_a_r)
    send_corr(0)

    keys = win[1, own, :]
    wait_for(stats.at[pl.ds(0, CHUNKS - 1)], sem_st_r)
    for k in arrival:
        if abs(k - REACH) == 2:
            wait_q(k)
        scores = dot(keys, win[0, part(k), :], NT) * SCALE
        pair_stats = stats[k]
        scores = jnp.where(valid(k), scores - pair_stats[0:1], LOW)
        weights = jnp.exp(scores) * pair_stats[1:2]
        probs_t[:, part(k)] = weights * SCALE
        probs_tb[:, part(k)] = weights.astype(BF16)

    gain_own = gain_v[:, pl.ds(pl.multiple_of(tp * cols, cols), cols)]

    def inner_row(a, b):
        row = jnp.sum(dif[a] * (kry[0] if b is None else dif[b]), axis=0, keepdims=True)
        folded = row[:, 0:HD]
        for start in range(HD, cols, HD):
            folded = folded + row[:, start : start + HD]
        return folded

    pairs = [(a, b) for a in range(SSTEP) for b in list(range(a + 1)) + [None]]

    def inner_rows(a):
        for place, (first, second) in enumerate(pairs):
            if first == a:
                tile[place : place + 1, :] = inner_row(first, second)

    tile[...] = jnp.zeros(tile.shape, F32)

    def product(n, carry):
        def give_back(t, whole):
            whole = whole.astype(BF16)
            first, second = whole[0:TOK], whole[TOK:CHIP]
            mine = core == 0
            g_full[n, core, t] = jnp.where(mine, first, second)
            g_swap[n, t] = jnp.where(mine, second, first)

        def both_heads(t):
            return jnp.concatenate([g_full[n, 0, t], g_full[n, 1, t]], axis=1)

        def tp_rows(o):
            return pl.ds(pl.multiple_of(tp_start[o], cols), cols)

        wait_for(g_win.at[n, pl.ds(0, TOK)], sem_g_r.at[n, REACH])
        grad = g_win[n, own, :]
        corr = jnp.sum(grad.astype(F32) * att_head[...], axis=1, keepdims=True)
        grad_q = jnp.zeros((CHIP, HD), F32)
        for k in range(CHUNKS):
            grad_p = dot(grad, win[2, part(k), :], NT)
            score = (probs[:, part(k)] * (grad_p - corr)).astype(BF16)
            grad_q = grad_q + dot(score, win[1, part(k), :], NN)
        give_back(0, grad_q)
        send(
            g_swap.at[n, pl.ds(0, 1)],
            g_full.at[n, core, pl.ds(0, 1)],
            sem_sw_s.at[n],
            sem_sw_r.at[n, 0],
            pair,
        )
        def key_side(k, values, wide, low):
            grad = g_win[n, span(k), :]
            corr = jnp.concatenate([c_win[n, 2 * k], c_win[n, 2 * k + 1]], axis=1)
            score = (wide * (dot(values, grad, NT) - corr)).astype(BF16)
            return dot(score, win[0, span(k), :], NN), dot(low, grad, NN)

        def wait_grad(k):
            mine = k is REACH
            if not mine:
                wait_for(g_win.at[n, pl.ds(0, CHIP)], sem_g_r.at[n, k])
            wait_for(c_win.at[n, pl.ds(0, 1 if mine else 2)], sem_c_r.at[n, k])

        for place, k in enumerate(soon):
            wait_grad(k)
            grad_k, grad_v = key_side(
                k, win[2, own, :], probs_t[:, span(k)], probs_tb[:, span(k)]
            )
            if place == 0:
                kv_acc[0] = grad_k
                kv_acc[1] = grad_v
                wait_for(g_swap.at[n, pl.ds(0, 1)], sem_sw_r.at[n, 0])
                for o in range(n_tp):
                    rs_acc[o] = dot(both_heads(0), w_q[tp_rows(o), :], NT)
            else:
                kv_acc[0] += grad_k
                kv_acc[1] += grad_v
        for k in last:
            wait_grad(k)
        for token_core in (other, core):
            taken = pl.ds(pl.multiple_of(token_core * TOK, TOK), TOK)
            window = pl.ds(pl.multiple_of(HALF + token_core * TOK, TOK), TOK)
            sums = [kv_acc[0, taken, :], kv_acc[1, taken, :]]
            for k in last:
                grad_k, grad_v = key_side(
                    k,
                    win[2, window, :],
                    probs_t[taken, span(k)],
                    probs_tb[taken, span(k)],
                )
                sums = [sums[0] + grad_k, sums[1] + grad_v]
            for t in range(2):
                if token_core is other:
                    g_swap[n, 1 + t] = sums[t].astype(BF16)
                else:
                    g_full[n, core, 1 + t] = sums[t].astype(BF16)
            if token_core is other:
                send(
                    g_swap.at[n, pl.ds(1, 2)],
                    g_full.at[n, core, pl.ds(1, 2)],
                    sem_sw_s.at[n],
                    sem_sw_r.at[n, 1],
                    pair,
                )

        def partial_sum(o, head):
            late = jnp.concatenate([g_full[n, head, 1], g_full[n, head, 2]], axis=1)
            return rs_acc[o] + dot(late, w_kv[head, tp_rows(o), :], NT)

        for o in range(n_tp):
            rs_acc[o] = partial_sum(o, core)
        wait_for(g_swap.at[n, pl.ds(1, 2)], sem_sw_r.at[n, 1])

        def send_sum(o, b):
            send(
                rs_send.at[n, o - 1, pl.ds(b * BT, BT)],
                rs_recv.at[n, o - 1, pl.ds(b * BT, BT)],
                sem_rs_s.at[n],
                sem_rs_r.at[n, b],
                tp_device[o],
            )

        for o in tp_far:
            rs_send[n, o - 1] = partial_sum(o, other).astype(BF16)
            send_sum(o, 0)
        for b in range(1, BLOCKS):
            for o in tp_far:
                send_sum(o, b)
        rs_acc[0] = partial_sum(0, other)
        for b, rows in enumerate(blocks):
            wait_for(
                rs_recv.at[n, pl.ds(0, n_tp - 1), pl.ds(0, BT)], sem_rs_r.at[n, b]
            )
            summed = rs_acc[0, rows, :]
            for o in range(1, n_tp):
                summed = summed + rs_recv[n, o - 1, rows, :].astype(F32)
            inverse = jnp.concatenate([inv_v[rows, :]] * (cols // HD), axis=1)
            vector = inverse * (gain_own * summed)

            @pl.when(n < SSTEP - 1)
            def _():
                xg[n + 1, tp, rows, :] = vector.astype(BF16)
                send_vector(n + 1, b)

            kry[n + 1, rows, :] = vector
            dif[n, rows, :] = kry[n, rows, :] - vector

        @pl.when(n < SSTEP - 1)
        def _():
            for b in range(GRAD_BLOCKS):
                send_grad_out(n + 1, b)
            send_corr(n + 1)

        for a in range(SSTEP):

            @pl.when(n == a)
            def _():
                inner_rows(a)

        return carry

    lax.fori_loop(0, SSTEP, product, 0)

    square = jnp.concatenate(
        [tile[...], jnp.zeros((HD - tile.shape[0], HD), F32)], axis=0
    )
    whole = jnp.sum(square.T, axis=0, keepdims=True)
    start = 0
    for stage, devices in enumerate((stage_a, stage_b)):
        rows_out[stage] = whole
        for k, device in enumerate(devices):
            send(
                rows_out.at[stage],
                rows_in.at[start + k],
                sem_t_s,
                sem_t_r.at[stage],
                device,
            )
        wait_for(rows_in.at[pl.ds(start, len(devices))], sem_t_r.at[stage])
        whole = whole + jnp.sum(rows_in[start : start + len(devices)], axis=0)
        start += len(devices)
    spread = jnp.broadcast_to(whole, (HD, HD)).T

    def inner(a, b):
        place = pairs.index((a, b))
        return spread[place : place + 1]

    factor = {}
    for a in range(SSTEP):
        for b in range(a + 1):
            value = inner(a, b)
            for c in range(b):
                value = value - factor[a, c] * factor[b, c]
            factor[a, b] = jnp.sqrt(value) if a == b else value / factor[b, b]
    half = []
    for a in range(SSTEP):
        value = inner(a, None)
        for b in range(a):
            value = value - factor[a, b] * half[b]
        half.append(value / factor[a, a])
    coef = [None] * SSTEP
    for a in range(SSTEP - 1, -1, -1):
        value = half[a]
        for b in range(a + 1, SSTEP):
            value = value - factor[b, a] * coef[b]
        coef[a] = value / factor[a, a]
    coef = [jnp.concatenate([c] * (cols // HD), axis=1) for c in coef]
    adjoint = coef[0] * kry[0]
    for n in range(1, SSTEP):
        adjoint = adjoint + coef[n] * kry[n]
    adj_out[...] = adjoint
    residual = kry[0]
    for n in range(SSTEP):
        residual = residual - coef[n] * dif[n]
    res_out[...] = residual

    sent = 4 * REACH + 1
    wait_for(xs.at[pl.ds(0, n_tp - 1)], sem_xs_s)
    wait_for(win.at[:, pl.ds(0, sent * TOK)], sem_q_s)
    wait_for(att_own.at[0], sem_a_s)
    wait_for(stats.at[pl.ds(0, CHUNKS - 1)], sem_st_s)
    for n in range(SSTEP):
        wait_for(xg.at[n, pl.ds(0, n_tp - 1)], sem_xg_s.at[n])
        wait_for(g_win.at[n, pl.ds(0, sent * TOK)], sem_g_s.at[n])
        wait_for(c_win.at[n, pl.ds(0, sent)], sem_c_s.at[n])
        wait_for(g_swap.at[n], sem_sw_s.at[n])
        wait_for(rs_send.at[n], sem_rs_s.at[n])
    wait_for(rows_in, sem_t_s)


def on_device(sizes, state, cotangent, norm_gain, w_query, w_key, w_value, w_out):
    n_seq, n_tp, n_y, n_z = sizes
    tok, cols = state.shape
    width = n_tp * cols
    row_count = (2 * n_y - 1) + (n_z * n_tp - 1)
    dma = pltpu.SemaphoreType.DMA
    scratch = [
        pltpu.VMEM((width, 2 * HD), BF16),
        pltpu.VMEM((2, width, 2 * HD), BF16),
        pltpu.VMEM((2 * HD, width), BF16),
        pltpu.VMEM((1, width), F32),
        pltpu.VMEM((n_tp, tok, cols), BF16),
        pltpu.VMEM((tok, width), BF16),
        pltpu.VMEM((SSTEP, n_tp, tok, cols), BF16),
        pltpu.VMEM((2, 3, tok, HD), BF16),
        pltpu.VMEM((3, SPAN, HD), BF16),
        pltpu.VMEM((CHIP, HD), F32),
        pltpu.VMEM((2, tok, HD), F32),
        pltpu.VMEM((CHUNKS, 8, CHIP), F32),
        pltpu.VMEM((CHIP, SPAN), F32),
        pltpu.VMEM((CHIP, SPAN), F32),
        pltpu.VMEM((CHIP, SPAN), BF16),
        pltpu.VMEM((SSTEP, 2, tok, HD), BF16),
        pltpu.VMEM((SSTEP, SPAN, HD), BF16),
        pltpu.VMEM((SSTEP, 2, 1, HD), F32),
        pltpu.VMEM((SSTEP, 2 * CHUNKS, 1, HD), F32),
        pltpu.VMEM((SSTEP, 2, 3, tok, HD), BF16),
        pltpu.VMEM((SSTEP, 3, tok, HD), BF16),
        pltpu.VMEM((2, CHIP, HD), F32),
        pltpu.VMEM((n_tp, tok, cols), F32),
        pltpu.VMEM((SSTEP, n_tp - 1, tok, cols), BF16),
        pltpu.VMEM((SSTEP, n_tp - 1, tok, cols), BF16),
        pltpu.VMEM((SSTEP + 1, tok, cols), F32),
        pltpu.VMEM((SSTEP, tok, cols), F32),
        pltpu.VMEM((tok, HD), F32),
        pltpu.VMEM((16, HD), F32),
        pltpu.VMEM((2, 1, HD), F32),
        pltpu.VMEM((row_count, 1, HD), F32),
        dma((9,)),
        dma,
        dma((BLOCKS,)),
        dma((SSTEP,)),
        dma((SSTEP, BLOCKS)),
        dma,
        dma((CHUNKS, BLOCKS)),
        dma((CHUNKS,)),
        dma,
        dma,
        dma,
        dma,
        dma((SSTEP,)),
        dma((SSTEP, CHUNKS)),
        dma((SSTEP,)),
        dma((SSTEP, CHUNKS)),
        dma((SSTEP,)),
        dma((SSTEP, 2)),
        dma((SSTEP,)),
        dma((SSTEP, BLOCKS)),
        dma,
        dma((2,)),
    ]
    anywhere = pl.BlockSpec(memory_space=pl.ANY)
    return pl.pallas_call(
        functools.partial(kernel, sizes),
        out_shape=(pltpu.VMEM((tok, cols), F32), pltpu.VMEM((tok, cols), F32)),
        in_specs=[anywhere] * 7,
        out_specs=(pl.BlockSpec(memory_space=pltpu.VMEM),) * 2,
        scratch_shapes=scratch,
        compiler_params=pltpu.CompilerParams(
            collective_id=0, has_side_effects=True, vmem_limit_bytes=63 * 2**20
        ),
        name="block",
    )(state, cotangent, norm_gain.reshape(1, width), w_query, w_key, w_value, w_out)


def solution(mesh):
    n_seq, n_tp = mesh.shape["seq"], mesh.shape["tp"]
    n_chip = n_seq // 2
    n_y = 1
    while n_y * n_y < n_chip:
        n_y *= 2
    sizes = (n_seq, n_tp, n_y, n_chip // n_y)
    in_specs = (
        P("seq", "tp"),
        P("seq", "tp"),
        P(),
        P(None, "tp"),
        P(None, "tp"),
        P(None, "tp"),
        P("tp", None),
    )
    return jax.shard_map(
        functools.partial(on_device, sizes),
        mesh=mesh,
        in_specs=in_specs,
        out_specs=(P("seq", "tp"), P("seq", "tp")),
        check_vma=False,
    )
```
